32 devices in a mesh: depth: 4 (over y, x), tile: 8 (over z, core).
Axes of the slice: x: 2, y: 2, z: 4, core: 2. Of those that a mesh axis runs over, the one named last changes fastest.
Arguments:
- volume: float32 [64, 512, 2048], P('depth', 'tile'), may hold values from -6 to 6
- entry_depth: int32 [512, 2048], P('tile'), may hold values from 0 to 31
- light_dir: float32 [3], replicated, may hold values from 0.2 to 1
- transfer: float32 [4, 3], replicated, may hold values from -6 to 6
Outputs:
- frame_rgba: float32 [4, 512, 2048], P(None, 'tile', 'depth')
The draws below stay inside these ranges and needn't reach their ends.
All inputs are finite; a program needn't handle non-finite values.
Results may differ from the reference program's by a relative error of at most 0.0003.
Values sent between devices are 32-bit elements; how exact they have to be, the bound alone decides.
A program may use at most 128 MiB of HBM per device.

```python
import jax
import jax.numpy as jnp
from jax import lax

TX = 64
NY = 2048
NZ = 64
NX = 512


def set_ends(values, own_key, least, high):
    index_at = [jax.random.randint(jax.random.fold_in(own_key, axis), (), 0, length) for axis, length in enumerate(values.shape)]
    longest = values.shape.index(max(values.shape))
    beside = index_at[:longest] + [(index_at[longest] + 1) % values.shape[longest]] + index_at[longest + 1:]
    return values.at[tuple(index_at)].set(least).at[tuple(beside)].set(high)


def block_scale(key, dims, cuts, least, high):
    def one(axis_at, blocks):
        draws = jax.random.uniform(jax.random.fold_in(jax.random.fold_in(key, 6), axis_at), (blocks,), jnp.float32, least / len(cuts), high / len(cuts))
        return jnp.repeat(jnp.exp(draws), dims[axis_at] // blocks).reshape((-1,) + (1,) * (len(dims) - axis_at - 1))

    level = one(*cuts[0])
    for cut in cuts[1:]:
        level = level * one(*cut)
    return level


def noise(rng, shape, width, limit, shards=(), kind=jnp.bfloat16):
    gain = block_scale(rng, shape, shards, -0.22, 0.18) if shards else 1.0
    values = jax.random.normal(rng, shape, jnp.float32) * width * gain
    return jnp.minimum(jnp.maximum(values, -limit), limit).astype(kind)


def setup_inputs(seed: int = 0) -> dict:
    streams_of = jax.random.split(jax.random.key(seed), 5)
    volume = noise(streams_of[0], (NZ, NX, NY), 1.0, 6.0, ((0, 4), (1, 8)), jnp.float32)
    entry_depth = set_ends(jax.random.randint(streams_of[1], (NX, NY), 0, NZ // 2), jax.random.fold_in(streams_of[1], 1), 0, (NZ // 2) - 1).astype(jnp.int32)
    light_dir = jnp.clip(jax.random.uniform(streams_of[2], (3,), jnp.float32, 0.2, 1.0), 0.2, 1.0)
    transfer = noise(streams_of[3], (4, 3), 1.5, 6.0, (), jnp.float32)
    return dict(volume=volume, entry_depth=entry_depth, light_dir=light_dir, transfer=transfer)


def emission(padded, depth_pos, entry_depth, light_dir, transfer, depth_total):
    centre = padded[1:-1, 1:-1, 1:-1]
    grad_z = (padded[2:, 1:-1, 1:-1] - padded[:-2, 1:-1, 1:-1]) * 0.5
    grad_x = (padded[1:-1, 2:, 1:-1] - padded[1:-1, :-2, 1:-1]) * 0.5
    grad_y = (padded[1:-1, 1:-1, 2:] - padded[1:-1, 1:-1, :-2]) * 0.5
    grad_norm = jnp.sqrt(grad_z * grad_z + grad_x * grad_x + grad_y * grad_y + 1.0)
    light_norm = jnp.sqrt(jnp.sum(light_dir * light_dir))
    facing = jnp.abs(light_dir[0] * grad_z + light_dir[1] * grad_x + light_dir[2] * grad_y)
    shading = 0.3 + 0.7 * facing / (grad_norm * light_norm)
    opacity = 4.0 / depth_total * jax.nn.sigmoid(transfer[3, 0] * centre + transfer[3, 1] * grad_norm + transfer[3, 2])
    opacity = jnp.where(depth_pos[:, None, None] >= entry_depth[None], opacity, 0.0)
    colors = jnp.stack([shading * jax.nn.sigmoid(transfer[k, 0] * centre + transfer[k, 1] * grad_norm + transfer[k, 2]) for k in range(3)])
    return (opacity, colors)

def composite(opacity, colors):
    logs = jnp.log1p(-opacity)
    transmit = jnp.exp(jnp.cumsum(logs, axis=0) - logs)
    weight = transmit * opacity
    shaded = lax.optimization_barrier(jnp.sum(weight[None] * colors, axis=1))
    return jnp.concatenate([shaded, lax.optimization_barrier(jnp.sum(weight, axis=0))[None]], axis=0)

def reference(volume, entry_depth, light_dir, transfer):
    padded = jnp.pad(volume, 1)
    depth_pos = jnp.arange(NZ, dtype=jnp.int32)

    def one_block(block):
        row_start = (block * TX).astype(jnp.int32)
        zero = jnp.zeros((), jnp.int32)
        piece = lax.dynamic_slice(padded, (zero, row_start, zero), (NZ + 2, TX + 2, NY + 2))
        entries = lax.dynamic_slice(entry_depth, (row_start, zero), (TX, NY))
        opacity, colors = emission(piece, depth_pos, entries, light_dir, transfer, float(NZ))
        return composite(opacity, colors)
    blocks = lax.map(one_block, jnp.arange(NX // TX, dtype=jnp.int32))
    return jnp.transpose(blocks, (1, 0, 2, 3)).reshape(4, NX, NY)
```

```python
import functools

import jax
import jax.numpy as jnp
from jax import lax
from jax.experimental import pallas as pl
from jax.experimental.pallas import tpu as pltpu
from jax.sharding import PartitionSpec as P

LANES = 128
PAD = 8
BLOCK = 32
LOG2E = 1.4426950408889634


def kernel(groups, tiles, depth_total, volume, entry, light, transfer, out, vol, top_out, bottom_out, top_in,
           bottom_in, sent, got, load_sem, front_sem, back_sem, row_sem, piece_send, piece_recv):
    slab, rows, columns = volume.shape
    strips = columns // LANES
    own = strips // groups
    me, tile = lax.axis_index("depth"), lax.axis_index("tile")
    body = pl.ds(PAD, rows)

    def load(strip):
        return pltpu.make_async_copy(
            volume.at[:, :, pl.ds(pl.multiple_of(strip * LANES, LANES), LANES)],
            vol.at[pl.ds(1, slab), strip + 1, body, :],
            load_sem.at[strip],
        )

    def front(strip):
        return pltpu.make_async_remote_copy(
            src_ref=volume.at[slab - 1, :, pl.ds(pl.multiple_of(strip * LANES, LANES), LANES)],
            dst_ref=vol.at[0, strip + 1, body, :],
            send_sem=front_sem.at[0, strip],
            recv_sem=front_sem.at[1, strip],
            device_id={"depth": lax.rem(me + 1, groups)},
            device_id_type=pl.DeviceIdType.MESH,
        )

    def back(strip):
        return pltpu.make_async_remote_copy(
            src_ref=volume.at[0, :, pl.ds(pl.multiple_of(strip * LANES, LANES), LANES)],
            dst_ref=vol.at[slab + 1, strip + 1, body, :],
            send_sem=back_sem.at[0, strip],
            recv_sem=back_sem.at[1, strip],
            device_id={"depth": lax.rem(me + groups - 1, groups)},
            device_id_type=pl.DeviceIdType.MESH,
        )

    def row_copy(src, dst, way, target):
        return pltpu.make_async_remote_copy(
            src_ref=src,
            dst_ref=dst,
            send_sem=row_sem.at[0, way],
            recv_sem=row_sem.at[1, way],
            device_id={"tile": target},
            device_id_type=pl.DeviceIdType.MESH,
        )

    def piece(strip, target, source, k):
        return pltpu.make_async_remote_copy(
            src_ref=sent.at[strip],
            dst_ref=got.at[source, k],
            send_sem=piece_send.at[strip],
            recv_sem=piece_recv.at[source, k],
            device_id={"depth": target},
            device_id_type=pl.DeviceIdType.MESH,
        )

    def strip_at(step, device):
        k = step // groups
        target = lax.rem(device + 1 + lax.rem(step, groups), groups)
        return target * own + k, target, k

    up, down = lax.rem(tile + tiles - 1, tiles), lax.rem(tile + 1, tiles)
    to_lower = row_copy(bottom_out, top_in, 0, down)
    to_upper = row_copy(top_out, bottom_in, 1, up)

    @pl.loop(0, strips)
    def _(strip):
        load(strip).start()

    barrier = pltpu.get_barrier_semaphore()
    for hop in range(1, groups):
        pl.semaphore_signal(barrier, inc=1, device_id={"depth": lax.rem(me + hop, groups)},
                            device_id_type=pl.DeviceIdType.MESH)
    for target in (up, down):
        pl.semaphore_signal(barrier, inc=1, device_id={"tile": target}, device_id_type=pl.DeviceIdType.MESH)
    pl.semaphore_wait(barrier, groups + 1)

    @pl.loop(0, strips)
    def _(step):
        @pl.when(me < groups - 1)
        def _():
            front(strip_at(step, me + 1)[0]).start()

        @pl.when(me > 0)
        def _():
            back(strip_at(step, me - 1 + groups)[0]).start()

    zeros = jnp.zeros((rows, LANES), jnp.float32)

    @pl.when(me == 0)
    def _():
        @pl.loop(0, strips)
        def _(strip):
            vol[0, strip + 1, body, :] = zeros

    @pl.when(me == groups - 1)
    def _():
        @pl.loop(0, strips)
        def _(strip):
            vol[slab + 1, strip + 1, body, :] = zeros

    @pl.loop(0, slab)
    def _(layer):
        vol[layer + 1, 0, body, :] = zeros
        vol[layer + 1, strips + 1, body, :] = zeros

    @pl.loop(0, strips)
    def _(strip):
        load(strip).wait()
        for layer in range(slab):
            top_out[strip, pl.ds(layer, 1), :] = vol[layer + 1, strip + 1, pl.ds(PAD, 1), :]
            bottom_out[strip, pl.ds(layer, 1), :] = vol[layer + 1, strip + 1, pl.ds(PAD + rows - 1, 1), :]

    @pl.when(tile < tiles - 1)
    def _():
        to_lower.start()

    @pl.when(tile > 0)
    def _():
        to_upper.start()

    @pl.when(tile == 0)
    def _():
        top_in[...] = jnp.zeros_like(top_in)

    @pl.when(tile == tiles - 1)
    def _():
        bottom_in[...] = jnp.zeros_like(bottom_in)

    @pl.when(tile > 0)
    def _():
        to_lower.wait_recv()

    @pl.when(tile < tiles - 1)
    def _():
        to_upper.wait_recv()

    @pl.loop(0, strips)
    def _(strip):
        for layer in range(slab):
            vol[layer + 1, strip + 1, pl.ds(PAD - 1, 1), :] = top_in[strip, pl.ds(layer, 1), :]
            vol[layer + 1, strip + 1, pl.ds(PAD + rows, 1), :] = bottom_in[strip, pl.ds(layer, 1), :]

    shape = (BLOCK, LANES)
    light_sq = light[0] * light[0] + light[1] * light[1] + light[2] * light[2]
    light_scale = 0.175 * lax.rsqrt(jnp.full(shape, light_sq, jnp.float32))
    light_z, light_x, light_y = (light[i] * light_scale for i in range(3))
    tone = [[0.5 * transfer[k, j] for j in range(3)] for k in range(3)]
    thick = [-LOG2E * transfer[3, j] for j in range(3)]
    lane = lax.broadcasted_iota(jnp.int32, shape, 1)
    first, last = lane == 0, lane == LANES - 1
    peak = 4.0 / depth_total

    @pl.loop(0, strips)
    def _(step):
        strip, target, k = strip_at(step, me)
        at = strip + 1

        @pl.when(me > 0)
        def _():
            front(strip).wait_recv()

        @pl.when(me < groups - 1)
        def _():
            back(strip).wait_recv()

        for low in range(0, rows, BLOCK):
            here = pl.ds(PAD + low, BLOCK)
            entered = entry[pl.ds(low, BLOCK), pl.ds(pl.multiple_of(strip * LANES, LANES), LANES)] - me * slab
            before, value = vol[0, at, here, :], vol[1, at, here, :]
            clear = jnp.ones(shape, jnp.float32)
            total = jnp.zeros(shape, jnp.float32)
            base = jnp.zeros(shape, jnp.float32)
            sums = [jnp.zeros(shape, jnp.float32)] * 3
            for layer in range(slab):
                after = vol[layer + 2, at, here, :]
                grad_z = after - before
                grad_x = vol[layer + 1, at, pl.ds(PAD + low + 1, BLOCK), :] - vol[
                    layer + 1, at, pl.ds(PAD + low - 1, BLOCK), :]
                right = jnp.where(first, vol[layer + 1, at + 1, here, :], value)
                left = jnp.where(last, vol[layer + 1, at - 1, here, :], value)
                grad_y = pltpu.roll(right, LANES - 1, 1) - pltpu.roll(left, 1, 1)
                square = 0.25 * (grad_z * grad_z + grad_x * grad_x + grad_y * grad_y) + 1.0
                inverse = lax.rsqrt(square)
                norm = square * inverse
                facing = jnp.abs(light_z * grad_z + light_x * grad_x + light_y * grad_y)
                half_shade = 0.15 + facing * inverse
                spread = 1.0 + jnp.exp2(jnp.minimum(thick[0] * value + thick[1] * norm + thick[2], 126.0))
                guess = pl.reciprocal(spread, approx=True)
                opacity = peak * (guess * (2.0 - spread * guess))
                opacity = jnp.where(entered <= layer, opacity, 0.0)
                weight = clear * opacity
                clear = clear - weight
                total = total + weight
                lit = weight * half_shade
                base = base + lit
                for c in range(3):
                    sums[c] = sums[c] + lit * jnp.tanh(tone[c][0] * value + tone[c][1] * norm + tone[c][2])
                before, value = value, after
            for c in range(3):
                sent[strip, c, pl.ds(low, BLOCK), :] = base + sums[c]
            sent[strip, 3, pl.ds(low, BLOCK), :] = total

        @pl.when(target != me)
        def _():
            piece(strip, target, me, k).start()

        @pl.when(target == me)
        def _():
            got[me, k] = sent[strip]

    for k in range(own):
        for hop in range(1, groups):
            source = lax.rem(me + hop, groups)
            piece(source * own + k, source, source, k).wait_recv()
        for low in range(0, rows, BLOCK):
            here = pl.ds(low, BLOCK)
            clear = jnp.ones(shape, jnp.float32)
            sums = [jnp.zeros(shape, jnp.float32)] * 4
            for source in range(groups):
                alpha = got[source, k, 3, here, :]
                for c in range(3):
                    sums[c] = sums[c] + clear * got[source, k, c, here, :]
                sums[3] = sums[3] + clear * alpha
                clear = clear - clear * alpha
            for c in range(4):
                out[c, here, pl.ds(k * LANES, LANES)] = sums[c]

    @pl.loop(0, strips)
    def _(step):
        strip, target, k = strip_at(step, me)

        @pl.when(me < groups - 1)
        def _():
            front(strip).wait_send()

        @pl.when(me > 0)
        def _():
            back(strip).wait_send()

        @pl.when(target != me)
        def _():
            piece(strip, target, me, k).wait_send()

    @pl.when(tile < tiles - 1)
    def _():
        to_lower.wait_send()

    @pl.when(tile > 0)
    def _():
        to_upper.wait_send()


def local(volume, entry_depth, light_dir, transfer):
    slab, rows, columns = volume.shape
    groups, tiles = lax.axis_size("depth"), lax.axis_size("tile")
    strips = columns // LANES
    own = strips // groups
    edge = pltpu.VMEM((strips, slab, LANES), jnp.float32)
    return pl.pallas_call(
        functools.partial(kernel, groups, tiles, float(slab * groups)),
        out_shape=jax.ShapeDtypeStruct((4, rows, columns // groups), jnp.float32),
        in_specs=[
            pl.BlockSpec(memory_space=pl.ANY),
            pl.BlockSpec(memory_space=pltpu.VMEM),
            pl.BlockSpec(memory_space=pltpu.SMEM),
            pl.BlockSpec(memory_space=pltpu.SMEM),
        ],
        out_specs=pl.BlockSpec(memory_space=pltpu.VMEM),
        scratch_shapes=[
            pltpu.VMEM((slab + 2, strips + 2, rows + 2 * PAD, LANES), jnp.float32),
            edge,
            edge,
            edge,
            edge,
            pltpu.VMEM((strips, 4, rows, LANES), jnp.float32),
            pltpu.VMEM((groups, own, 4, rows, LANES), jnp.float32),
            pltpu.SemaphoreType.DMA((strips,)),
            pltpu.SemaphoreType.DMA((2, strips)),
            pltpu.SemaphoreType.DMA((2, strips)),
            pltpu.SemaphoreType.DMA((2, 2)),
            pltpu.SemaphoreType.DMA((strips,)),
            pltpu.SemaphoreType.DMA((groups, own)),
        ],
        compiler_params=pltpu.CompilerParams(
            collective_id=0, has_side_effects=True, vmem_limit_bytes=40 * 1024 * 1024
        ),
        cost_estimate=pl.CostEstimate(
            flops=60 * slab * rows * columns, bytes_accessed=4 * slab * rows * columns, transcendentals=6 * slab * rows * columns
        ),
    )(volume, entry_depth, light_dir, transfer)


def solution(mesh):
    placed = (P("depth", "tile", None), P("tile", None), P(), P())
    return jax.shard_map(
        local, mesh=mesh, in_specs=placed, out_specs=P(None, "tile", "depth"), check_vma=False
    )
```

```python
import functools

import jax
import jax.numpy as jnp
from jax import lax
from jax.experimental import pallas as pl
from jax.experimental.pallas import tpu as pltpu
from jax.sharding import PartitionSpec as P

LANES = 128
PAD = 8
BLOCK = 32
LOG2E = 1.4426950408889634


def kernel(groups, tiles, depth_total, volume, entry_hbm, light_hbm, transfer_hbm, out, entry, light, transfer, vol, top_out, bottom_out, top_in,
           bottom_in, sent, got, small_sem, load_sem, front_sem, back_sem, row_sem, piece_send, piece_recv):
    slab, rows, columns = volume.shape
    strips = columns // LANES
    own = strips // groups
    me, tile = lax.axis_index("depth"), lax.axis_index("tile")
    body = pl.ds(PAD, rows)

    def load(strip):
        return pltpu.make_async_copy(
            volume.at[:, :, pl.ds(pl.multiple_of(strip * LANES, LANES), LANES)],
            vol.at[pl.ds(1, slab), strip + 1, body, :],
            load_sem.at[strip],
        )

    def front(strip):
        return pltpu.make_async_remote_copy(
            src_ref=volume.at[slab - 1, :, pl.ds(pl.multiple_of(strip * LANES, LANES), LANES)],
            dst_ref=vol.at[0, strip + 1, body, :],
            send_sem=front_sem.at[0, strip],
            recv_sem=front_sem.at[1, strip],
            device_id={"depth": lax.rem(me + 1, groups)},
            device_id_type=pl.DeviceIdType.MESH,
        )

    def back(strip):
        return pltpu.make_async_remote_copy(
            src_ref=volume.at[0, :, pl.ds(pl.multiple_of(strip * LANES, LANES), LANES)],
            dst_ref=vol.at[slab + 1, strip + 1, body, :],
            send_sem=back_sem.at[0, strip],
            recv_sem=back_sem.at[1, strip],
            device_id={"depth": lax.rem(me + groups - 1, groups)},
            device_id_type=pl.DeviceIdType.MESH,
        )

    def row_copy(src, dst, way, target):
        return pltpu.make_async_remote_copy(
            src_ref=src,
            dst_ref=dst,
            send_sem=row_sem.at[0, way],
            recv_sem=row_sem.at[1, way],
            device_id={"tile": target},
            device_id_type=pl.DeviceIdType.MESH,
        )

    def piece(strip, target, source, k):
        return pltpu.make_async_remote_copy(
            src_ref=sent.at[strip],
            dst_ref=got.at[source, k],
            send_sem=piece_send.at[strip],
            recv_sem=piece_recv.at[source, k],
            device_id={"depth": target},
            device_id_type=pl.DeviceIdType.MESH,
        )

    def strip_at(step, device):
        k = step // groups
        target = lax.rem(device + 1 + lax.rem(step, groups), groups)
        return target * own + k, target, k

    up, down = lax.rem(tile + tiles - 1, tiles), lax.rem(tile + 1, tiles)
    to_lower = row_copy(bottom_out, top_in, 0, down)
    to_upper = row_copy(top_out, bottom_in, 1, up)

    small = [
        pltpu.make_async_copy(src, dst, small_sem.at[i])
        for i, (src, dst) in enumerate(((entry_hbm, entry), (light_hbm, light), (transfer_hbm, transfer)))
    ]

    @pl.loop(0, strips)
    def _(strip):
        load(strip).start()

    for copy in small:
        copy.start()

    barrier = pltpu.get_barrier_semaphore()
    for hop in range(1, groups):
        pl.semaphore_signal(barrier, inc=1, device_id={"depth": lax.rem(me + hop, groups)},
                            device_id_type=pl.DeviceIdType.MESH)
    for target in (up, down):
        pl.semaphore_signal(barrier, inc=1, device_id={"tile": target}, device_id_type=pl.DeviceIdType.MESH)
    pl.semaphore_wait(barrier, groups + 1)

    @pl.loop(0, strips)
    def _(step):
        @pl.when(me < groups - 1)
        def _():
            front(strip_at(step, me + 1)[0]).start()

        @pl.when(me > 0)
        def _():
            back(strip_at(step, me - 1 + groups)[0]).start()

    zeros = jnp.zeros((rows, LANES), jnp.float32)

    @pl.when(me == 0)
    def _():
        @pl.loop(0, strips)
        def _(strip):
            vol[0, strip + 1, body, :] = zeros

    @pl.when(me == groups - 1)
    def _():
        @pl.loop(0, strips)
        def _(strip):
            vol[slab + 1, strip + 1, body, :] = zeros

    @pl.loop(0, slab)
    def _(layer):
        vol[layer + 1, 0, body, :] = zeros
        vol[layer + 1, strips + 1, body, :] = zeros

    @pl.loop(0, strips)
    def _(strip):
        load(strip).wait()
        for layer in range(slab):
            top_out[strip, pl.ds(layer, 1), :] = vol[layer + 1, strip + 1, pl.ds(PAD, 1), :]
            bottom_out[strip, pl.ds(layer, 1), :] = vol[layer + 1, strip + 1, pl.ds(PAD + rows - 1, 1), :]

    @pl.when(tile < tiles - 1)
    def _():
        to_lower.start()

    @pl.when(tile > 0)
    def _():
        to_upper.start()

    @pl.when(tile == 0)
    def _():
        top_in[...] = jnp.zeros_like(top_in)

    @pl.when(tile == tiles - 1)
    def _():
        bottom_in[...] = jnp.zeros_like(bottom_in)

    @pl.when(tile > 0)
    def _():
        to_lower.wait_recv()

    @pl.when(tile < tiles - 1)
    def _():
        to_upper.wait_recv()

    @pl.loop(0, strips)
    def _(strip):
        for layer in range(slab):
            vol[layer + 1, strip + 1, pl.ds(PAD - 1, 1), :] = top_in[strip, pl.ds(layer, 1), :]
            vol[layer + 1, strip + 1, pl.ds(PAD + rows, 1), :] = bottom_in[strip, pl.ds(layer, 1), :]

    for copy in small:
        copy.wait()

    shape = (BLOCK, LANES)
    light_sq = light[0] * light[0] + light[1] * light[1] + light[2] * light[2]
    light_scale = 0.175 * lax.rsqrt(jnp.full(shape, light_sq, jnp.float32))
    light_z, light_x, light_y = (light[i] * light_scale for i in range(3))
    tone = [[0.5 * transfer[k, j] for j in range(3)] for k in range(3)]
    thick = [-LOG2E * transfer[3, j] for j in range(3)]
    lane = lax.broadcasted_iota(jnp.int32, shape, 1)
    first, last = lane == 0, lane == LANES - 1
    peak = 4.0 / depth_total

    @pl.loop(0, strips)
    def _(step):
        strip, target, k = strip_at(step, me)
        at = strip + 1

        @pl.when(me > 0)
        def _():
            front(strip).wait_recv()

        @pl.when(me < groups - 1)
        def _():
            back(strip).wait_recv()

        for low in range(0, rows, BLOCK):
            here = pl.ds(PAD + low, BLOCK)
            entered = entry[pl.ds(low, BLOCK), pl.ds(pl.multiple_of(strip * LANES, LANES), LANES)] - me * slab
            before, value = vol[0, at, here, :], vol[1, at, here, :]
            clear = jnp.ones(shape, jnp.float32)
            total = jnp.zeros(shape, jnp.float32)
            base = jnp.zeros(shape, jnp.float32)
            sums = [jnp.zeros(shape, jnp.float32)] * 3
            for layer in range(slab):
                after = vol[layer + 2, at, here, :]
                grad_z = after - before
                grad_x = vol[layer + 1, at, pl.ds(PAD + low + 1, BLOCK), :] - vol[
                    layer + 1, at, pl.ds(PAD + low - 1, BLOCK), :]
                right = jnp.where(first, vol[layer + 1, at + 1, here, :], value)
                left = jnp.where(last, vol[layer + 1, at - 1, here, :], value)
                grad_y = pltpu.roll(right, LANES - 1, 1) - pltpu.roll(left, 1, 1)
                square = 0.25 * (grad_z * grad_z + grad_x * grad_x + grad_y * grad_y) + 1.0
                inverse = lax.rsqrt(square)
                norm = square * inverse
                facing = jnp.abs(light_z * grad_z + light_x * grad_x + light_y * grad_y)
                half_shade = 0.15 + facing * inverse
                spread = 1.0 + jnp.exp2(jnp.minimum(thick[0] * value + thick[1] * norm + thick[2], 126.0))
                guess = pl.reciprocal(spread, approx=True)
                opacity = peak * (guess * (2.0 - spread * guess))
                opacity = jnp.where(entered <= layer, opacity, 0.0)
                weight = clear * opacity
                clear = clear - weight
                total = total + weight
                lit = weight * half_shade
                base = base + lit
                for c in range(3):
                    sums[c] = sums[c] + lit * jnp.tanh(tone[c][0] * value + tone[c][1] * norm + tone[c][2])
                before, value = value, after
            for c in range(3):
                sent[strip, c, pl.ds(low, BLOCK), :] = base + sums[c]
            sent[strip, 3, pl.ds(low, BLOCK), :] = total

        @pl.when(target != me)
        def _():
            piece(strip, target, me, k).start()

        @pl.when(target == me)
        def _():
            got[me, k] = sent[strip]

    for k in range(own):
        for hop in range(1, groups):
            source = lax.rem(me + hop, groups)
            piece(source * own + k, source, source, k).wait_recv()
        for low in range(0, rows, BLOCK):
            here = pl.ds(low, BLOCK)
            clear = jnp.ones(shape, jnp.float32)
            sums = [jnp.zeros(shape, jnp.float32)] * 4
            for source in range(groups):
                alpha = got[source, k, 3, here, :]
                for c in range(3):
                    sums[c] = sums[c] + clear * got[source, k, c, here, :]
                sums[3] = sums[3] + clear * alpha
                clear = clear - clear * alpha
            for c in range(4):
                out[c, here, pl.ds(k * LANES, LANES)] = sums[c]

    @pl.loop(0, strips)
    def _(step):
        strip, target, k = strip_at(step, me)

        @pl.when(me < groups - 1)
        def _():
            front(strip).wait_send()

        @pl.when(me > 0)
        def _():
            back(strip).wait_send()

        @pl.when(target != me)
        def _():
            piece(strip, target, me, k).wait_send()

    @pl.when(tile < tiles - 1)
    def _():
        to_lower.wait_send()

    @pl.when(tile > 0)
    def _():
        to_upper.wait_send()


def local(volume, entry_depth, light_dir, transfer):
    slab, rows, columns = volume.shape
    groups, tiles = lax.axis_size("depth"), lax.axis_size("tile")
    strips = columns // LANES
    own = strips // groups
    edge = pltpu.VMEM((strips, slab, LANES), jnp.float32)
    return pl.pallas_call(
        functools.partial(kernel, groups, tiles, float(slab * groups)),
        out_shape=jax.ShapeDtypeStruct((4, rows, columns // groups), jnp.float32),
        in_specs=[pl.BlockSpec(memory_space=pl.ANY)] * 4,
        out_specs=pl.BlockSpec(memory_space=pltpu.VMEM),
        scratch_shapes=[
            pltpu.VMEM((rows, columns), jnp.int32),
            pltpu.SMEM((3,), jnp.float32),
            pltpu.SMEM((4, 3), jnp.float32),
            pltpu.VMEM((slab + 2, strips + 2, rows + 2 * PAD, LANES), jnp.float32),
            edge,
            edge,
            edge,
            edge,
            pltpu.VMEM((strips, 4, rows, LANES), jnp.float32),
            pltpu.VMEM((groups, own, 4, rows, LANES), jnp.float32),
            pltpu.SemaphoreType.DMA((3,)),
            pltpu.SemaphoreType.DMA((strips,)),
            pltpu.SemaphoreType.DMA((2, strips)),
            pltpu.SemaphoreType.DMA((2, strips)),
            pltpu.SemaphoreType.DMA((2, 2)),
            pltpu.SemaphoreType.DMA((strips,)),
            pltpu.SemaphoreType.DMA((groups, own)),
        ],
        compiler_params=pltpu.CompilerParams(
            collective_id=0, has_side_effects=True, vmem_limit_bytes=60 * 1024 * 1024
        ),
        cost_estimate=pl.CostEstimate(
            flops=60 * slab * rows * columns, bytes_accessed=4 * slab * rows * columns, transcendentals=6 * slab * rows * columns
        ),
    )(volume, entry_depth, light_dir, transfer)


def solution(mesh):
    placed = (P("depth", "tile", None), P("tile", None), P(), P())
    return jax.shard_map(
        local, mesh=mesh, in_specs=placed, out_specs=P(None, "tile", "depth"), check_vma=False
    )
```

```python
import functools

import jax
import jax.numpy as jnp
from jax import lax
from jax.experimental import pallas as pl
from jax.experimental.pallas import tpu as pltpu
from jax.sharding import PartitionSpec as P

LANES = 128
PAD = 8
BLOCK = 32
LOG2E = 1.4426950408889634


def kernel(groups, tiles, depth_total, volume, entry_hbm, light_hbm, transfer_hbm, out, entry, light, transfer, vol, top_out, bottom_out, top_in,
           bottom_in, sent, got, passing, small_sem, load_sem, front_sem, back_sem, row_sem, piece_send, piece_recv, pass_send, pass_recv):
    slab, rows, columns = volume.shape
    strips = columns // LANES
    own = strips // groups
    me, tile = lax.axis_index("depth"), lax.axis_index("tile")
    body = pl.ds(PAD, rows)

    def load(strip):
        return pltpu.make_async_copy(
            volume.at[:, :, pl.ds(pl.multiple_of(strip * LANES, LANES), LANES)],
            vol.at[pl.ds(1, slab), strip + 1, body, :],
            load_sem.at[strip],
        )

    def front(strip):
        return pltpu.make_async_remote_copy(
            src_ref=volume.at[slab - 1, :, pl.ds(pl.multiple_of(strip * LANES, LANES), LANES)],
            dst_ref=vol.at[0, strip + 1, body, :],
            send_sem=front_sem.at[0, strip],
            recv_sem=front_sem.at[1, strip],
            device_id={"depth": lax.rem(me + 1, groups)},
            device_id_type=pl.DeviceIdType.MESH,
        )

    def back(strip):
        return pltpu.make_async_remote_copy(
            src_ref=volume.at[0, :, pl.ds(pl.multiple_of(strip * LANES, LANES), LANES)],
            dst_ref=vol.at[slab + 1, strip + 1, body, :],
            send_sem=back_sem.at[0, strip],
            recv_sem=back_sem.at[1, strip],
            device_id={"depth": lax.rem(me + groups - 1, groups)},
            device_id_type=pl.DeviceIdType.MESH,
        )

    def row_copy(src, dst, way, target):
        return pltpu.make_async_remote_copy(
            src_ref=src,
            dst_ref=dst,
            send_sem=row_sem.at[0, way],
            recv_sem=row_sem.at[1, way],
            device_id={"tile": target},
            device_id_type=pl.DeviceIdType.MESH,
        )

    def piece(strip, target, source, k):
        return pltpu.make_async_remote_copy(
            src_ref=sent.at[strip],
            dst_ref=got.at[source, k],
            send_sem=piece_send.at[strip],
            recv_sem=piece_recv.at[source, k],
            device_id={"depth": target},
            device_id_type=pl.DeviceIdType.MESH,
        )

    relays = own // 2 if groups == 4 else 0
    middle = jnp.logical_and(me > 0, me < groups - 1)

    def pass_in(strip, k):
        return pltpu.make_async_remote_copy(
            src_ref=sent.at[strip],
            dst_ref=passing.at[k],
            send_sem=piece_send.at[strip],
            recv_sem=pass_recv.at[k],
            device_id={"depth": lax.rem(me + 2, groups)},
            device_id_type=pl.DeviceIdType.MESH,
        )

    def pass_on(k):
        target = jnp.where(me == 0, 1, 2)
        source = 3 - target
        return pltpu.make_async_remote_copy(
            src_ref=passing.at[k],
            dst_ref=got.at[source, k],
            send_sem=pass_send.at[k],
            recv_sem=piece_recv.at[source, k],
            device_id={"depth": target},
            device_id_type=pl.DeviceIdType.MESH,
        )

    def strip_at(step, device):
        k = step // groups
        target = lax.rem(device + 1 + lax.rem(step, groups), groups)
        return target * own + k, target, k

    up, down = lax.rem(tile + tiles - 1, tiles), lax.rem(tile + 1, tiles)
    to_lower = row_copy(bottom_out, top_in, 0, down)
    to_upper = row_copy(top_out, bottom_in, 1, up)

    small = [
        pltpu.make_async_copy(src, dst, small_sem.at[i])
        for i, (src, dst) in enumerate(((entry_hbm, entry), (light_hbm, light), (transfer_hbm, transfer)))
    ]

    @pl.loop(0, strips)
    def _(strip):
        load(strip).start()

    for copy in small:
        copy.start()

    barrier = pltpu.get_barrier_semaphore()
    for hop in range(1, groups):
        pl.semaphore_signal(barrier, inc=1, device_id={"depth": lax.rem(me + hop, groups)},
                            device_id_type=pl.DeviceIdType.MESH)
    for target in (up, down):
        pl.semaphore_signal(barrier, inc=1, device_id={"tile": target}, device_id_type=pl.DeviceIdType.MESH)
    pl.semaphore_wait(barrier, groups + 1)

    @pl.loop(0, strips)
    def _(step):
        @pl.when(me < groups - 1)
        def _():
            front(strip_at(step, me + 1)[0]).start()

        @pl.when(me > 0)
        def _():
            back(strip_at(step, me - 1 + groups)[0]).start()

    zeros = jnp.zeros((rows, LANES), jnp.float32)

    @pl.when(me == 0)
    def _():
        @pl.loop(0, strips)
        def _(strip):
            vol[0, strip + 1, body, :] = zeros

    @pl.when(me == groups - 1)
    def _():
        @pl.loop(0, strips)
        def _(strip):
            vol[slab + 1, strip + 1, body, :] = zeros

    @pl.loop(0, slab)
    def _(layer):
        vol[layer + 1, 0, body, :] = zeros
        vol[layer + 1, strips + 1, body, :] = zeros

    @pl.loop(0, strips)
    def _(strip):
        load(strip).wait()
        for layer in range(slab):
            top_out[strip, pl.ds(layer, 1), :] = vol[layer + 1, strip + 1, pl.ds(PAD, 1), :]
            bottom_out[strip, pl.ds(layer, 1), :] = vol[layer + 1, strip + 1, pl.ds(PAD + rows - 1, 1), :]

    @pl.when(tile < tiles - 1)
    def _():
        to_lower.start()

    @pl.when(tile > 0)
    def _():
        to_upper.start()

    @pl.when(tile == 0)
    def _():
        top_in[...] = jnp.zeros_like(top_in)

    @pl.when(tile == tiles - 1)
    def _():
        bottom_in[...] = jnp.zeros_like(bottom_in)

    @pl.when(tile > 0)
    def _():
        to_lower.wait_recv()

    @pl.when(tile < tiles - 1)
    def _():
        to_upper.wait_recv()

    @pl.loop(0, strips)
    def _(strip):
        for layer in range(slab):
            vol[layer + 1, strip + 1, pl.ds(PAD - 1, 1), :] = top_in[strip, pl.ds(layer, 1), :]
            vol[layer + 1, strip + 1, pl.ds(PAD + rows, 1), :] = bottom_in[strip, pl.ds(layer, 1), :]

    for copy in small:
        copy.wait()

    shape = (BLOCK, LANES)
    light_sq = light[0] * light[0] + light[1] * light[1] + light[2] * light[2]
    light_scale = 0.175 * lax.rsqrt(jnp.full(shape, light_sq, jnp.float32))
    light_z, light_x, light_y = (light[i] * light_scale for i in range(3))
    tone = [[0.5 * transfer[k, j] for j in range(3)] for k in range(3)]
    thick = [-LOG2E * transfer[3, j] for j in range(3)]
    lane = lax.broadcasted_iota(jnp.int32, shape, 1)
    first, last = lane == 0, lane == LANES - 1
    peak = 4.0 / depth_total

    @pl.loop(0, strips)
    def _(step):
        strip, target, k = strip_at(step, me)
        at = strip + 1

        @pl.when(me > 0)
        def _():
            front(strip).wait_recv()

        @pl.when(me < groups - 1)
        def _():
            back(strip).wait_recv()

        for low in range(0, rows, BLOCK):
            here = pl.ds(PAD + low, BLOCK)
            entered = entry[pl.ds(low, BLOCK), pl.ds(pl.multiple_of(strip * LANES, LANES), LANES)] - me * slab
            before, value = vol[0, at, here, :], vol[1, at, here, :]
            clear = jnp.ones(shape, jnp.float32)
            total = jnp.zeros(shape, jnp.float32)
            base = jnp.zeros(shape, jnp.float32)
            sums = [jnp.zeros(shape, jnp.float32)] * 3
            for layer in range(slab):
                after = vol[layer + 2, at, here, :]
                grad_z = after - before
                grad_x = vol[layer + 1, at, pl.ds(PAD + low + 1, BLOCK), :] - vol[
                    layer + 1, at, pl.ds(PAD + low - 1, BLOCK), :]
                right = jnp.where(first, vol[layer + 1, at + 1, here, :], value)
                left = jnp.where(last, vol[layer + 1, at - 1, here, :], value)
                grad_y = pltpu.roll(right, LANES - 1, 1) - pltpu.roll(left, 1, 1)
                square = 0.25 * (grad_z * grad_z + grad_x * grad_x + grad_y * grad_y) + 1.0
                inverse = lax.rsqrt(square)
                norm = square * inverse
                facing = jnp.abs(light_z * grad_z + light_x * grad_x + light_y * grad_y)
                half_shade = 0.15 + facing * inverse
                spread = 1.0 + jnp.exp2(jnp.minimum(thick[0] * value + thick[1] * norm + thick[2], 126.0))
                guess = pl.reciprocal(spread, approx=True)
                opacity = peak * (guess * (2.0 - spread * guess))
                opacity = jnp.where(entered <= layer, opacity, 0.0)
                weight = clear * opacity
                clear = clear - weight
                total = total + weight
                lit = weight * half_shade
                base = base + lit
                for c in range(3):
                    sums[c] = sums[c] + lit * jnp.tanh(tone[c][0] * value + tone[c][1] * norm + tone[c][2])
                before, value = value, after
            for c in range(3):
                sent[strip, c, pl.ds(low, BLOCK), :] = base + sums[c]
            sent[strip, 3, pl.ds(low, BLOCK), :] = total

        relayed = jnp.logical_and(jnp.logical_and(middle, target == 3 - me), k < relays)

        @pl.when(jnp.logical_and(target != me, jnp.logical_not(relayed)))
        def _():
            piece(strip, target, me, k).start()

        if relays:
            @pl.when(relayed)
            def _():
                pass_in(strip, k).start()

            @pl.when(jnp.logical_and(jnp.logical_not(middle), jnp.logical_and(lax.rem(step, groups) == 0, k >= own - relays)))
            def _():
                pass_in(strip, k - (own - relays)).wait_recv()
                pass_on(k - (own - relays)).start()

        @pl.when(target == me)
        def _():
            got[me, k] = sent[strip]

    for k in range(own):
        for hop in range(1, groups):
            source = lax.rem(me + hop, groups)
            piece(source * own + k, source, source, k).wait_recv()
        for low in range(0, rows, BLOCK):
            here = pl.ds(low, BLOCK)
            clear = jnp.ones(shape, jnp.float32)
            sums = [jnp.zeros(shape, jnp.float32)] * 4
            for source in range(groups):
                alpha = got[source, k, 3, here, :]
                for c in range(3):
                    sums[c] = sums[c] + clear * got[source, k, c, here, :]
                sums[3] = sums[3] + clear * alpha
                clear = clear - clear * alpha
            for c in range(4):
                out[c, here, pl.ds(k * LANES, LANES)] = sums[c]

    @pl.loop(0, strips)
    def _(step):
        strip, target, k = strip_at(step, me)

        @pl.when(me < groups - 1)
        def _():
            front(strip).wait_send()

        @pl.when(me > 0)
        def _():
            back(strip).wait_send()

        @pl.when(target != me)
        def _():
            piece(strip, target, me, k).wait_send()

    if relays:
        @pl.when(jnp.logical_not(middle))
        def _():
            for k in range(relays):
                pass_on(k).wait_send()

    @pl.when(tile < tiles - 1)
    def _():
        to_lower.wait_send()

    @pl.when(tile > 0)
    def _():
        to_upper.wait_send()


def local(volume, entry_depth, light_dir, transfer):
    slab, rows, columns = volume.shape
    groups, tiles = lax.axis_size("depth"), lax.axis_size("tile")
    strips = columns // LANES
    own = strips // groups
    edge = pltpu.VMEM((strips, slab, LANES), jnp.float32)
    return pl.pallas_call(
        functools.partial(kernel, groups, tiles, float(slab * groups)),
        out_shape=jax.ShapeDtypeStruct((4, rows, columns // groups), jnp.float32),
        in_specs=[pl.BlockSpec(memory_space=pltpu.HBM)] * 4,
        out_specs=pl.BlockSpec(memory_space=pltpu.VMEM),
        scratch_shapes=[
            pltpu.VMEM((rows, columns), jnp.int32),
            pltpu.SMEM((3,), jnp.float32),
            pltpu.SMEM((4, 3), jnp.float32),
            pltpu.VMEM((slab + 2, strips + 2, rows + 2 * PAD, LANES), jnp.float32),
            edge,
            edge,
            edge,
            edge,
            pltpu.VMEM((strips, 4, rows, LANES), jnp.float32),
            pltpu.VMEM((groups, own, 4, rows, LANES), jnp.float32),
            pltpu.VMEM((max(own // 2, 1), 4, rows, LANES), jnp.float32),
            pltpu.SemaphoreType.DMA((3,)),
            pltpu.SemaphoreType.DMA((strips,)),
            pltpu.SemaphoreType.DMA((2, strips)),
            pltpu.SemaphoreType.DMA((2, strips)),
            pltpu.SemaphoreType.DMA((2, 2)),
            pltpu.SemaphoreType.DMA((strips,)),
            pltpu.SemaphoreType.DMA((groups, own)),
            pltpu.SemaphoreType.DMA((max(own // 2, 1),)),
            pltpu.SemaphoreType.DMA((max(own // 2, 1),)),
        ],
        compiler_params=pltpu.CompilerParams(
            collective_id=0, has_side_effects=True, vmem_limit_bytes=40 * 1024 * 1024
        ),
        cost_estimate=pl.CostEstimate(
            flops=60 * slab * rows * columns, bytes_accessed=4 * slab * rows * columns, transcendentals=6 * slab * rows * columns
        ),
    )(volume, entry_depth, light_dir, transfer)


def solution(mesh):
    placed = (P("depth", "tile", None), P("tile", None), P(), P())
    return jax.shard_map(
        local, mesh=mesh, in_specs=placed, out_specs=P(None, "tile", "depth"), check_vma=False
    )
```

```python
import functools

import jax
import jax.numpy as jnp
from jax import lax
from jax.experimental import pallas as pl
from jax.experimental.pallas import tpu as pltpu
from jax.sharding import PartitionSpec as P

LANES = 128
PAD = 8
BLOCK = 32
LOG2E = 1.4426950408889634


def kernel(groups, tiles, depth_total, volume, entry_hbm, light_hbm, transfer_hbm, out, entry, light, transfer, vol, top_out, bottom_out, top_in,
           bottom_in, sent, got, passing, small_sem, load_sem, front_sem, back_sem, row_sem, piece_send, piece_recv, pass_send, pass_recv):
    slab, rows, columns = volume.shape
    strips = columns // LANES
    own = strips // groups
    me, tile = lax.axis_index("depth"), lax.axis_index("tile")
    body = pl.ds(PAD, rows)

    def load(strip):
        return pltpu.make_async_copy(
            volume.at[:, :, pl.ds(pl.multiple_of(strip * LANES, LANES), LANES)],
            vol.at[pl.ds(1, slab), strip + 1, body, :],
            load_sem.at[strip],
        )

    def front(strip):
        return pltpu.make_async_remote_copy(
            src_ref=volume.at[slab - 1, :, pl.ds(pl.multiple_of(strip * LANES, LANES), LANES)],
            dst_ref=vol.at[0, strip + 1, body, :],
            send_sem=front_sem.at[0, strip],
            recv_sem=front_sem.at[1, strip],
            device_id={"depth": lax.rem(me + 1, groups)},
            device_id_type=pl.DeviceIdType.MESH,
        )

    def back(strip):
        return pltpu.make_async_remote_copy(
            src_ref=volume.at[0, :, pl.ds(pl.multiple_of(strip * LANES, LANES), LANES)],
            dst_ref=vol.at[slab + 1, strip + 1, body, :],
            send_sem=back_sem.at[0, strip],
            recv_sem=back_sem.at[1, strip],
            device_id={"depth": lax.rem(me + groups - 1, groups)},
            device_id_type=pl.DeviceIdType.MESH,
        )

    def row_copy(src, dst, way, target):
        return pltpu.make_async_remote_copy(
            src_ref=src,
            dst_ref=dst,
            send_sem=row_sem.at[0, way],
            recv_sem=row_sem.at[1, way],
            device_id={"tile": target},
            device_id_type=pl.DeviceIdType.MESH,
        )

    def piece(strip, target, source, k):
        return pltpu.make_async_remote_copy(
            src_ref=sent.at[strip],
            dst_ref=got.at[source, k],
            send_sem=piece_send.at[strip],
            recv_sem=piece_recv.at[source, k],
            device_id={"depth": target},
            device_id_type=pl.DeviceIdType.MESH,
        )

    relays = own // 2 if groups == 4 else 0
    middle = jnp.logical_and(me > 0, me < groups - 1)

    def pass_in(strip, k):
        return pltpu.make_async_remote_copy(
            src_ref=sent.at[strip],
            dst_ref=passing.at[k],
            send_sem=piece_send.at[strip],
            recv_sem=pass_recv.at[k],
            device_id={"depth": lax.rem(me + 2, groups)},
            device_id_type=pl.DeviceIdType.MESH,
        )

    def pass_on(k):
        target = jnp.where(me == 0, 1, 2)
        source = 3 - target
        return pltpu.make_async_remote_copy(
            src_ref=passing.at[k],
            dst_ref=got.at[source, k],
            send_sem=pass_send.at[k],
            recv_sem=piece_recv.at[source, k],
            device_id={"depth": target},
            device_id_type=pl.DeviceIdType.MESH,
        )

    def strip_at(step, device):
        k = step // groups
        target = lax.rem(device + 1 + lax.rem(step, groups), groups)
        return target * own + k, target, k

    up, down = lax.rem(tile + tiles - 1, tiles), lax.rem(tile + 1, tiles)
    to_lower = row_copy(bottom_out, top_in, 0, down)
    to_upper = row_copy(top_out, bottom_in, 1, up)

    small = [
        pltpu.make_async_copy(src, dst, small_sem.at[i])
        for i, (src, dst) in enumerate(((entry_hbm, entry), (light_hbm, light), (transfer_hbm, transfer)))
    ]

    @pl.loop(0, strips)
    def _(strip):
        load(strip).start()

    for copy in small:
        copy.start()

    barrier = pltpu.get_barrier_semaphore()
    for hop in range(1, groups):
        pl.semaphore_signal(barrier, inc=1, device_id={"depth": lax.rem(me + hop, groups)},
                            device_id_type=pl.DeviceIdType.MESH)
    for target in (up, down):
        pl.semaphore_signal(barrier, inc=1, device_id={"tile": target}, device_id_type=pl.DeviceIdType.MESH)
    pl.semaphore_wait(barrier, groups + 1)

    @pl.loop(0, strips)
    def _(step):
        @pl.when(me < groups - 1)
        def _():
            front(strip_at(step, me + 1)[0]).start()

        @pl.when(me > 0)
        def _():
            back(strip_at(step, me - 1 + groups)[0]).start()

    zeros = jnp.zeros((rows, LANES), jnp.float32)

    @pl.when(me == 0)
    def _():
        @pl.loop(0, strips)
        def _(strip):
            vol[0, strip + 1, body, :] = zeros

    @pl.when(me == groups - 1)
    def _():
        @pl.loop(0, strips)
        def _(strip):
            vol[slab + 1, strip + 1, body, :] = zeros

    @pl.loop(0, slab)
    def _(layer):
        vol[layer + 1, 0, body, :] = zeros
        vol[layer + 1, strips + 1, body, :] = zeros

    @pl.loop(0, strips)
    def _(strip):
        load(strip).wait()
        for layer in range(slab):
            top_out[strip, pl.ds(layer, 1), :] = vol[layer + 1, strip + 1, pl.ds(PAD, 1), :]
            bottom_out[strip, pl.ds(layer, 1), :] = vol[layer + 1, strip + 1, pl.ds(PAD + rows - 1, 1), :]

    @pl.when(tile < tiles - 1)
    def _():
        to_lower.start()

    @pl.when(tile > 0)
    def _():
        to_upper.start()

    @pl.when(tile == 0)
    def _():
        top_in[...] = jnp.zeros_like(top_in)

    @pl.when(tile == tiles - 1)
    def _():
        bottom_in[...] = jnp.zeros_like(bottom_in)

    @pl.when(tile > 0)
    def _():
        to_lower.wait_recv()

    @pl.when(tile < tiles - 1)
    def _():
        to_upper.wait_recv()

    @pl.loop(0, strips)
    def _(strip):
        for layer in range(slab):
            vol[layer + 1, strip + 1, pl.ds(PAD - 1, 1), :] = top_in[strip, pl.ds(layer, 1), :]
            vol[layer + 1, strip + 1, pl.ds(PAD + rows, 1), :] = bottom_in[strip, pl.ds(layer, 1), :]

    for copy in small:
        copy.wait()

    shape = (BLOCK, LANES)
    light_sq = light[0] * light[0] + light[1] * light[1] + light[2] * light[2]
    light_scale = 0.175 * lax.rsqrt(jnp.full(shape, light_sq, jnp.float32))
    light_z, light_x, light_y = (light[i] * light_scale for i in range(3))
    tone = [[0.5 * transfer[k, j] for j in range(3)] for k in range(3)]
    thick = [-LOG2E * transfer[3, j] for j in range(3)]
    lane = lax.broadcasted_iota(jnp.int32, shape, 1)
    first, last = lane == 0, lane == LANES - 1
    peak = 4.0 / depth_total

    @pl.loop(0, strips)
    def _(step):
        strip, target, k = strip_at(step, me)
        at = strip + 1

        @pl.when(me > 0)
        def _():
            front(strip).wait_recv()

        @pl.when(me < groups - 1)
        def _():
            back(strip).wait_recv()

        for low in range(0, rows, BLOCK):
            here = pl.ds(PAD + low, BLOCK)
            entered = entry[pl.ds(low, BLOCK), pl.ds(pl.multiple_of(strip * LANES, LANES), LANES)] - me * slab
            before, value = vol[0, at, here, :], vol[1, at, here, :]
            clear = jnp.ones(shape, jnp.float32)
            total = jnp.zeros(shape, jnp.float32)
            base = jnp.zeros(shape, jnp.float32)
            sums = [jnp.zeros(shape, jnp.float32)] * 3
            for layer in range(slab):
                after = vol[layer + 2, at, here, :]
                grad_z = after - before
                grad_x = vol[layer + 1, at, pl.ds(PAD + low + 1, BLOCK), :] - vol[
                    layer + 1, at, pl.ds(PAD + low - 1, BLOCK), :]
                right = jnp.where(first, vol[layer + 1, at + 1, here, :], value)
                left = jnp.where(last, vol[layer + 1, at - 1, here, :], value)
                grad_y = pltpu.roll(right, LANES - 1, 1) - pltpu.roll(left, 1, 1)
                square = 0.25 * (grad_z * grad_z + grad_x * grad_x + grad_y * grad_y) + 1.0
                inverse = lax.rsqrt(square)
                norm = square * inverse
                facing = jnp.abs(light_z * grad_z + light_x * grad_x + light_y * grad_y)
                half_shade = 0.15 + facing * inverse
                spread = 1.0 + jnp.exp2(jnp.minimum(thick[0] * value + thick[1] * norm + thick[2], 126.0))
                guess = pl.reciprocal(spread, approx=True)
                opacity = peak * (guess * (2.0 - spread * guess))
                opacity = jnp.where(entered <= layer, opacity, 0.0)
                weight = clear * opacity
                clear = clear - weight
                total = total + weight
                lit = weight * half_shade
                base = base + lit
                for c in range(3):
                    sums[c] = sums[c] + lit * jnp.tanh(tone[c][0] * value + tone[c][1] * norm + tone[c][2])
                before, value = value, after
            for c in range(3):
                sent[strip, c, pl.ds(low, BLOCK), :] = base + sums[c]
            sent[strip, 3, pl.ds(low, BLOCK), :] = total

        relayed = jnp.logical_and(jnp.logical_and(middle, target == 3 - me), k < relays)

        @pl.when(jnp.logical_and(target != me, jnp.logical_not(relayed)))
        def _():
            piece(strip, target, me, k).start()

        if relays:
            @pl.when(relayed)
            def _():
                pass_in(strip, k).start()

            @pl.when(jnp.logical_and(jnp.logical_not(middle), jnp.logical_and(lax.rem(step, groups) == 0, k >= own - relays)))
            def _():
                pass_in(strip, k - (own - relays)).wait_recv()
                pass_on(k - (own - relays)).start()

        @pl.when(target == me)
        def _():
            got[me, k] = sent[strip]

    for k in range(own):
        for hop in range(1, groups):
            source = lax.rem(me + hop, groups)
            piece(source * own + k, source, source, k).wait_recv()
        for low in range(0, rows, BLOCK):
            here = pl.ds(low, BLOCK)
            clear = jnp.ones(shape, jnp.float32)
            sums = [jnp.zeros(shape, jnp.float32)] * 4
            for source in range(groups):
                alpha = got[source, k, 3, here, :]
                for c in range(3):
                    sums[c] = sums[c] + clear * got[source, k, c, here, :]
                sums[3] = sums[3] + clear * alpha
                clear = clear - clear * alpha
            for c in range(4):
                out[c, here, pl.ds(k * LANES, LANES)] = sums[c]

    @pl.loop(0, strips)
    def _(step):
        strip, target, k = strip_at(step, me)

        @pl.when(me < groups - 1)
        def _():
            front(strip).wait_send()

        @pl.when(me > 0)
        def _():
            back(strip).wait_send()

        @pl.when(target != me)
        def _():
            piece(strip, target, me, k).wait_send()

    if relays:
        @pl.when(jnp.logical_not(middle))
        def _():
            for k in range(relays):
                pass_on(k).wait_send()

    @pl.when(tile < tiles - 1)
    def _():
        to_lower.wait_send()

    @pl.when(tile > 0)
    def _():
        to_upper.wait_send()


def local(volume, entry_depth, light_dir, transfer):
    slab, rows, columns = volume.shape
    groups, tiles = lax.axis_size("depth"), lax.axis_size("tile")
    strips = columns // LANES
    own = strips // groups
    edge = pltpu.VMEM((strips, slab, LANES), jnp.float32)
    return pl.pallas_call(
        functools.partial(kernel, groups, tiles, float(slab * groups)),
        out_shape=jax.ShapeDtypeStruct((4, rows, columns // groups), jnp.float32),
        in_specs=[pl.BlockSpec(memory_space=pl.ANY)] * 4,
        out_specs=pl.BlockSpec(memory_space=pltpu.VMEM),
        scratch_shapes=[
            pltpu.VMEM((rows, columns), jnp.int32),
            pltpu.SMEM((3,), jnp.float32),
            pltpu.SMEM((4, 3), jnp.float32),
            pltpu.VMEM((slab + 2, strips + 2, rows + 2 * PAD, LANES), jnp.float32),
            edge,
            edge,
            edge,
            edge,
            pltpu.VMEM((strips, 4, rows, LANES), jnp.float32),
            pltpu.VMEM((groups, own, 4, rows, LANES), jnp.float32),
            pltpu.VMEM((max(own // 2, 1), 4, rows, LANES), jnp.float32),
            pltpu.SemaphoreType.DMA((3,)),
            pltpu.SemaphoreType.DMA((strips,)),
            pltpu.SemaphoreType.DMA((2, strips)),
            pltpu.SemaphoreType.DMA((2, strips)),
            pltpu.SemaphoreType.DMA((2, 2)),
            pltpu.SemaphoreType.DMA((strips,)),
            pltpu.SemaphoreType.DMA((groups, own)),
            pltpu.SemaphoreType.DMA((max(own // 2, 1),)),
            pltpu.SemaphoreType.DMA((max(own // 2, 1),)),
        ],
        compiler_params=pltpu.CompilerParams(
            collective_id=0, has_side_effects=True, vmem_limit_bytes=60 * 1024 * 1024
        ),
        cost_estimate=pl.CostEstimate(
            flops=60 * slab * rows * columns, bytes_accessed=4 * slab * rows * columns, transcendentals=6 * slab * rows * columns
        ),
    )(volume, entry_depth, light_dir, transfer)


def solution(mesh):
    placed = (P("depth", "tile", None), P("tile", None), P(), P())
    return jax.shard_map(
        local, mesh=mesh, in_specs=placed, out_specs=P(None, "tile", "depth"), check_vma=False
    )
```

```python
import functools

import jax
import jax.numpy as jnp
from jax import lax
from jax.experimental import pallas as pl
from jax.experimental.pallas import tpu as pltpu
from jax.sharding import PartitionSpec as P

LANES = 128
PAD = 8
BLOCK = 32
LOG2E = 1.4426950408889634


def kernel(groups, tiles, depth_total, volume, entry_hbm, light_hbm, transfer_hbm, out, entry, light, transfer, vol, top_out, bottom_out, top_in,
           bottom_in, sent, got, passing, small_sem, load_sem, front_sem, back_sem, row_sem, piece_send, piece_recv, pass_send, pass_recv):
    slab, rows, columns = volume.shape
    strips = columns // LANES
    own = strips // groups
    me, tile = lax.axis_index("depth"), lax.axis_index("tile")
    body = pl.ds(PAD, rows)

    def load(strip):
        return pltpu.make_async_copy(
            volume.at[:, :, pl.ds(pl.multiple_of(strip * LANES, LANES), LANES)],
            vol.at[pl.ds(1, slab), strip + 1, body, :],
            load_sem.at[strip],
        )

    def front(strip):
        return pltpu.make_async_remote_copy(
            src_ref=volume.at[slab - 1, :, pl.ds(pl.multiple_of(strip * LANES, LANES), LANES)],
            dst_ref=vol.at[0, strip + 1, body, :],
            send_sem=front_sem.at[0, strip],
            recv_sem=front_sem.at[1, strip],
            device_id={"depth": lax.rem(me + 1, groups)},
            device_id_type=pl.DeviceIdType.MESH,
        )

    def back(strip):
        return pltpu.make_async_remote_copy(
            src_ref=volume.at[0, :, pl.ds(pl.multiple_of(strip * LANES, LANES), LANES)],
            dst_ref=vol.at[slab + 1, strip + 1, body, :],
            send_sem=back_sem.at[0, strip],
            recv_sem=back_sem.at[1, strip],
            device_id={"depth": lax.rem(me + groups - 1, groups)},
            device_id_type=pl.DeviceIdType.MESH,
        )

    def row_copy(src, dst, way, target):
        return pltpu.make_async_remote_copy(
            src_ref=src,
            dst_ref=dst,
            send_sem=row_sem.at[0, way],
            recv_sem=row_sem.at[1, way],
            device_id={"tile": target},
            device_id_type=pl.DeviceIdType.MESH,
        )

    def piece(strip, target, source, k):
        return pltpu.make_async_remote_copy(
            src_ref=sent.at[strip],
            dst_ref=got.at[source, k],
            send_sem=piece_send.at[strip],
            recv_sem=piece_recv.at[source, k],
            device_id={"depth": target},
            device_id_type=pl.DeviceIdType.MESH,
        )

    relays = own // 2 if groups == 4 else 0
    middle = jnp.logical_and(me > 0, me < groups - 1)

    def pass_in(strip, k):
        return pltpu.make_async_remote_copy(
            src_ref=sent.at[strip],
            dst_ref=passing.at[k],
            send_sem=piece_send.at[strip],
            recv_sem=pass_recv.at[k],
            device_id={"depth": lax.rem(me + 2, groups)},
            device_id_type=pl.DeviceIdType.MESH,
        )

    def pass_on(k):
        target = jnp.where(me == 0, 1, 2)
        source = 3 - target
        return pltpu.make_async_remote_copy(
            src_ref=passing.at[k],
            dst_ref=got.at[source, k],
            send_sem=pass_send.at[k],
            recv_sem=piece_recv.at[source, k],
            device_id={"depth": target},
            device_id_type=pl.DeviceIdType.MESH,
        )

    def strip_at(step, device):
        others = groups - 1
        away = step < own * others
        k = jnp.where(away, step // others, step - own * others)
        target = lax.rem(device + jnp.where(away, 1 + lax.rem(step, others), 0), groups)
        return target * own + k, target, k

    up, down = lax.rem(tile + tiles - 1, tiles), lax.rem(tile + 1, tiles)
    to_lower = row_copy(bottom_out, top_in, 0, down)
    to_upper = row_copy(top_out, bottom_in, 1, up)

    small = [
        pltpu.make_async_copy(src, dst, small_sem.at[i])
        for i, (src, dst) in enumerate(((entry_hbm, entry), (light_hbm, light), (transfer_hbm, transfer)))
    ]

    @pl.loop(0, strips)
    def _(strip):
        load(strip).start()

    for copy in small:
        copy.start()

    barrier = pltpu.get_barrier_semaphore()
    for hop in range(1, groups):
        pl.semaphore_signal(barrier, inc=1, device_id={"depth": lax.rem(me + hop, groups)},
                            device_id_type=pl.DeviceIdType.MESH)
    for target in (up, down):
        pl.semaphore_signal(barrier, inc=1, device_id={"tile": target}, device_id_type=pl.DeviceIdType.MESH)
    pl.semaphore_wait(barrier, groups + 1)

    @pl.loop(0, strips)
    def _(step):
        @pl.when(me < groups - 1)
        def _():
            front(strip_at(step, me + 1)[0]).start()

        @pl.when(me > 0)
        def _():
            back(strip_at(step, me - 1 + groups)[0]).start()

    zeros = jnp.zeros((rows, LANES), jnp.float32)

    @pl.when(me == 0)
    def _():
        @pl.loop(0, strips)
        def _(strip):
            vol[0, strip + 1, body, :] = zeros

    @pl.when(me == groups - 1)
    def _():
        @pl.loop(0, strips)
        def _(strip):
            vol[slab + 1, strip + 1, body, :] = zeros

    @pl.loop(0, slab)
    def _(layer):
        vol[layer + 1, 0, body, :] = zeros
        vol[layer + 1, strips + 1, body, :] = zeros

    @pl.loop(0, strips)
    def _(strip):
        load(strip).wait()
        for layer in range(slab):
            top_out[strip, pl.ds(layer, 1), :] = vol[layer + 1, strip + 1, pl.ds(PAD, 1), :]
            bottom_out[strip, pl.ds(layer, 1), :] = vol[layer + 1, strip + 1, pl.ds(PAD + rows - 1, 1), :]

    @pl.when(tile < tiles - 1)
    def _():
        to_lower.start()

    @pl.when(tile > 0)
    def _():
        to_upper.start()

    @pl.when(tile == 0)
    def _():
        top_in[...] = jnp.zeros_like(top_in)

    @pl.when(tile == tiles - 1)
    def _():
        bottom_in[...] = jnp.zeros_like(bottom_in)

    @pl.when(tile > 0)
    def _():
        to_lower.wait_recv()

    @pl.when(tile < tiles - 1)
    def _():
        to_upper.wait_recv()

    @pl.loop(0, strips)
    def _(strip):
        for layer in range(slab):
            vol[layer + 1, strip + 1, pl.ds(PAD - 1, 1), :] = top_in[strip, pl.ds(layer, 1), :]
            vol[layer + 1, strip + 1, pl.ds(PAD + rows, 1), :] = bottom_in[strip, pl.ds(layer, 1), :]

    for copy in small:
        copy.wait()

    shape = (BLOCK, LANES)
    light_sq = light[0] * light[0] + light[1] * light[1] + light[2] * light[2]
    light_scale = 0.175 * lax.rsqrt(jnp.full(shape, light_sq, jnp.float32))
    light_z, light_x, light_y = (light[i] * light_scale for i in range(3))
    tone = [[0.5 * transfer[k, j] for j in range(3)] for k in range(3)]
    thick = [-LOG2E * transfer[3, j] for j in range(3)]
    lane = lax.broadcasted_iota(jnp.int32, shape, 1)
    first, last = lane == 0, lane == LANES - 1
    peak = 4.0 / depth_total

    @pl.loop(0, strips)
    def _(step):
        strip, target, k = strip_at(step, me)
        at = strip + 1

        @pl.when(me > 0)
        def _():
            front(strip).wait_recv()

        @pl.when(me < groups - 1)
        def _():
            back(strip).wait_recv()

        for low in range(0, rows, BLOCK):
            here = pl.ds(PAD + low, BLOCK)
            entered = entry[pl.ds(low, BLOCK), pl.ds(pl.multiple_of(strip * LANES, LANES), LANES)] - me * slab
            before, value = vol[0, at, here, :], vol[1, at, here, :]
            clear = jnp.ones(shape, jnp.float32)
            total = jnp.zeros(shape, jnp.float32)
            base = jnp.zeros(shape, jnp.float32)
            sums = [jnp.zeros(shape, jnp.float32)] * 3
            for layer in range(slab):
                after = vol[layer + 2, at, here, :]
                grad_z = after - before
                grad_x = vol[layer + 1, at, pl.ds(PAD + low + 1, BLOCK), :] - vol[
                    layer + 1, at, pl.ds(PAD + low - 1, BLOCK), :]
                right = jnp.where(first, vol[layer + 1, at + 1, here, :], value)
                left = jnp.where(last, vol[layer + 1, at - 1, here, :], value)
                grad_y = pltpu.roll(right, LANES - 1, 1) - pltpu.roll(left, 1, 1)
                square = 0.25 * (grad_z * grad_z + grad_x * grad_x + grad_y * grad_y) + 1.0
                inverse = lax.rsqrt(square)
                norm = square * inverse
                facing = jnp.abs(light_z * grad_z + light_x * grad_x + light_y * grad_y)
                half_shade = 0.15 + facing * inverse
                spread = 1.0 + jnp.exp2(jnp.minimum(thick[0] * value + thick[1] * norm + thick[2], 126.0))
                guess = pl.reciprocal(spread, approx=True)
                opacity = peak * (guess * (2.0 - spread * guess))
                opacity = jnp.where(entered <= layer, opacity, 0.0)
                weight = clear * opacity
                clear = clear - weight
                total = total + weight
                lit = weight * half_shade
                base = base + lit
                for c in range(3):
                    sums[c] = sums[c] + lit * jnp.tanh(tone[c][0] * value + tone[c][1] * norm + tone[c][2])
                before, value = value, after
            for c in range(3):
                sent[strip, c, pl.ds(low, BLOCK), :] = base + sums[c]
            sent[strip, 3, pl.ds(low, BLOCK), :] = total

        relayed = jnp.logical_and(jnp.logical_and(middle, target == 3 - me), k < relays)

        @pl.when(jnp.logical_and(target != me, jnp.logical_not(relayed)))
        def _():
            piece(strip, target, me, k).start()

        if relays:
            @pl.when(relayed)
            def _():
                pass_in(strip, k).start()

            @pl.when(jnp.logical_and(jnp.logical_not(middle), jnp.logical_and(target == lax.rem(me + 1, groups), k >= own - relays)))
            def _():
                pass_in(strip, k - (own - relays)).wait_recv()
                pass_on(k - (own - relays)).start()

        @pl.when(target == me)
        def _():
            got[me, k] = sent[strip]

    for k in range(own):
        for hop in range(1, groups):
            source = lax.rem(me + hop, groups)
            piece(source * own + k, source, source, k).wait_recv()
        for low in range(0, rows, BLOCK):
            here = pl.ds(low, BLOCK)
            clear = jnp.ones(shape, jnp.float32)
            sums = [jnp.zeros(shape, jnp.float32)] * 4
            for source in range(groups):
                alpha = got[source, k, 3, here, :]
                for c in range(3):
                    sums[c] = sums[c] + clear * got[source, k, c, here, :]
                sums[3] = sums[3] + clear * alpha
                clear = clear - clear * alpha
            for c in range(4):
                out[c, here, pl.ds(k * LANES, LANES)] = sums[c]

    @pl.loop(0, strips)
    def _(step):
        strip, target, k = strip_at(step, me)

        @pl.when(me < groups - 1)
        def _():
            front(strip).wait_send()

        @pl.when(me > 0)
        def _():
            back(strip).wait_send()

        @pl.when(target != me)
        def _():
            piece(strip, target, me, k).wait_send()

    if relays:
        @pl.when(jnp.logical_not(middle))
        def _():
            for k in range(relays):
                pass_on(k).wait_send()

    @pl.when(tile < tiles - 1)
    def _():
        to_lower.wait_send()

    @pl.when(tile > 0)
    def _():
        to_upper.wait_send()


def local(volume, entry_depth, light_dir, transfer):
    slab, rows, columns = volume.shape
    groups, tiles = lax.axis_size("depth"), lax.axis_size("tile")
    strips = columns // LANES
    own = strips // groups
    edge = pltpu.VMEM((strips, slab, LANES), jnp.float32)
    return pl.pallas_call(
        functools.partial(kernel, groups, tiles, float(slab * groups)),
        out_shape=jax.ShapeDtypeStruct((4, rows, columns // groups), jnp.float32),
        in_specs=[pl.BlockSpec(memory_space=pl.ANY)] * 4,
        out_specs=pl.BlockSpec(memory_space=pltpu.VMEM),
        scratch_shapes=[
            pltpu.VMEM((rows, columns), jnp.int32),
            pltpu.SMEM((3,), jnp.float32),
            pltpu.SMEM((4, 3), jnp.float32),
            pltpu.VMEM((slab + 2, strips + 2, rows + 2 * PAD, LANES), jnp.float32),
            edge,
            edge,
            edge,
            edge,
            pltpu.VMEM((strips, 4, rows, LANES), jnp.float32),
            pltpu.VMEM((groups, own, 4, rows, LANES), jnp.float32),
            pltpu.VMEM((max(own // 2, 1), 4, rows, LANES), jnp.float32),
            pltpu.SemaphoreType.DMA((3,)),
            pltpu.SemaphoreType.DMA((strips,)),
            pltpu.SemaphoreType.DMA((2, strips)),
            pltpu.SemaphoreType.DMA((2, strips)),
            pltpu.SemaphoreType.DMA((2, 2)),
            pltpu.SemaphoreType.DMA((strips,)),
            pltpu.SemaphoreType.DMA((groups, own)),
            pltpu.SemaphoreType.DMA((max(own // 2, 1),)),
            pltpu.SemaphoreType.DMA((max(own // 2, 1),)),
        ],
        compiler_params=pltpu.CompilerParams(
            collective_id=0, has_side_effects=True, vmem_limit_bytes=60 * 1024 * 1024
        ),
        cost_estimate=pl.CostEstimate(
            flops=60 * slab * rows * columns, bytes_accessed=4 * slab * rows * columns, transcendentals=6 * slab * rows * columns
        ),
    )(volume, entry_depth, light_dir, transfer)


def solution(mesh):
    placed = (P("depth", "tile", None), P("tile", None), P(), P())
    return jax.shard_map(
        local, mesh=mesh, in_specs=placed, out_specs=P(None, "tile", "depth"), check_vma=False
    )
```

```python
import functools

import jax
import jax.numpy as jnp
from jax import lax
from jax.experimental import pallas as pl
from jax.experimental.pallas import tpu as pltpu
from jax.sharding import PartitionSpec as P

LANES = 128
PAD = 8
BLOCK = 32
LOG2E = 1.4426950408889634


def kernel(groups, tiles, depth_total, volume, entry_hbm, light_hbm, transfer_hbm, out, entry, light, transfer, vol, top_out, bottom_out, top_in,
           bottom_in, sent, got, passing, between, merged, small_sem, load_sem, front_sem, back_sem, row_sem, piece_send, piece_recv, pass_recv, alpha_sem, merged_sem):
    slab, rows, columns = volume.shape
    strips = columns // LANES
    own = strips // groups
    me, tile = lax.axis_index("depth"), lax.axis_index("tile")
    body = pl.ds(PAD, rows)

    def load(strip):
        return pltpu.make_async_copy(
            volume.at[:, :, pl.ds(pl.multiple_of(strip * LANES, LANES), LANES)],
            vol.at[pl.ds(1, slab), strip + 1, body, :],
            load_sem.at[strip],
        )

    def front(strip):
        return pltpu.make_async_remote_copy(
            src_ref=volume.at[slab - 1, :, pl.ds(pl.multiple_of(strip * LANES, LANES), LANES)],
            dst_ref=vol.at[0, strip + 1, body, :],
            send_sem=front_sem.at[0, strip],
            recv_sem=front_sem.at[1, strip],
            device_id={"depth": lax.rem(me + 1, groups)},
            device_id_type=pl.DeviceIdType.MESH,
        )

    def back(strip):
        return pltpu.make_async_remote_copy(
            src_ref=volume.at[0, :, pl.ds(pl.multiple_of(strip * LANES, LANES), LANES)],
            dst_ref=vol.at[slab + 1, strip + 1, body, :],
            send_sem=back_sem.at[0, strip],
            recv_sem=back_sem.at[1, strip],
            device_id={"depth": lax.rem(me + groups - 1, groups)},
            device_id_type=pl.DeviceIdType.MESH,
        )

    def row_copy(src, dst, way, target):
        return pltpu.make_async_remote_copy(
            src_ref=src,
            dst_ref=dst,
            send_sem=row_sem.at[0, way],
            recv_sem=row_sem.at[1, way],
            device_id={"tile": target},
            device_id_type=pl.DeviceIdType.MESH,
        )

    def piece(strip, target, source, k):
        return pltpu.make_async_remote_copy(
            src_ref=sent.at[strip],
            dst_ref=got.at[source, k],
            send_sem=piece_send.at[strip],
            recv_sem=piece_recv.at[source, k],
            device_id={"depth": target},
            device_id_type=pl.DeviceIdType.MESH,
        )

    four = groups == 4
    mate, across, diagonal = me + 1 - 2 * lax.rem(me, 2), lax.rem(me + 2, groups), 3 - me
    middle = jnp.logical_and(me > 0, me < groups - 1)
    outer = jnp.logical_not(middle)

    def pass_in(strip, k):
        return pltpu.make_async_remote_copy(
            src_ref=sent.at[strip],
            dst_ref=passing.at[k],
            send_sem=piece_send.at[strip],
            recv_sem=pass_recv.at[k],
            device_id={"depth": across},
            device_id_type=pl.DeviceIdType.MESH,
        )

    def alpha_copy(k):
        return pltpu.make_async_remote_copy(
            src_ref=sent.at[me * own + k, 3],
            dst_ref=between.at[k],
            send_sem=alpha_sem.at[0, k],
            recv_sem=alpha_sem.at[1, k],
            device_id={"depth": mate},
            device_id_type=pl.DeviceIdType.MESH,
        )

    def merged_copy(k, target):
        return pltpu.make_async_remote_copy(
            src_ref=merged.at[k, pl.ds(0, 4)],
            dst_ref=got.at[target - 1, k],
            send_sem=merged_sem.at[0, k],
            recv_sem=piece_recv.at[target - 1, k],
            device_id={"depth": target},
            device_id_type=pl.DeviceIdType.MESH,
        )

    def later_copy(k, target):
        return pltpu.make_async_remote_copy(
            src_ref=merged.at[k, pl.ds(4, 1)],
            dst_ref=got.at[target + 1, k, pl.ds(3, 1)],
            send_sem=merged_sem.at[1, k],
            recv_sem=piece_recv.at[target + 1, k],
            device_id={"depth": target},
            device_id_type=pl.DeviceIdType.MESH,
        )

    def merge(k):
        pass_in(mate * own + k, k).wait_recv()
        alpha_copy(k).wait_recv()

        def combine(front_part, back_part):
            for low in range(0, rows, BLOCK):
                here = pl.ds(low, BLOCK)
                alpha = front_part[3, here, :]
                clear = (1.0 - alpha) * (1.0 - between[k, here, :])
                for c in range(3):
                    merged[k, c, here, :] = front_part[c, here, :] + clear * back_part[c, here, :]
                merged[k, 3, here, :] = alpha
                merged[k, 4, here, :] = back_part[3, here, :]

        @pl.when(me == 0)
        def _():
            combine(sent.at[mate * own + k], passing.at[k])

        @pl.when(me != 0)
        def _():
            combine(passing.at[k], sent.at[mate * own + k])

        merged_copy(k, mate).start()
        later_copy(k, mate).start()

    def route(target):
        if not four:
            no = target != target
            return target != me, no, no
        passed = jnp.logical_and(middle, target == diagonal)
        kept = jnp.logical_and(outer, target == mate)
        direct = jnp.logical_and(target != me, jnp.logical_not(jnp.logical_or(passed, kept)))
        return direct, passed, jnp.logical_and(middle, target == me)

    def strip_at(step, device):
        k, turn = step // groups, lax.rem(step, groups)
        if four:
            device = lax.rem(device, groups)
            beside = device + 1 - 2 * lax.rem(device, 2)
            opposite = lax.rem(device + 2, groups)
            inner = jnp.logical_and(device > 0, device < groups - 1)
            target = jnp.where(
                turn == 0,
                jnp.where(inner, 3 - device, beside),
                jnp.where(
                    turn == 1,
                    jnp.where(inner, device, 3 - device),
                    jnp.where(turn == 2, opposite, jnp.where(inner, beside, device)),
                ),
            )
        else:
            target = lax.rem(device + 1 + turn, groups)
        return target * own + k, target, k

    up, down = lax.rem(tile + tiles - 1, tiles), lax.rem(tile + 1, tiles)
    to_lower = row_copy(bottom_out, top_in, 0, down)
    to_upper = row_copy(top_out, bottom_in, 1, up)

    small = [
        pltpu.make_async_copy(src, dst, small_sem.at[i])
        for i, (src, dst) in enumerate(((entry_hbm, entry), (light_hbm, light), (transfer_hbm, transfer)))
    ]

    @pl.loop(0, strips)
    def _(strip):
        load(strip).start()

    for copy in small:
        copy.start()

    barrier = pltpu.get_barrier_semaphore()
    for hop in range(1, groups):
        pl.semaphore_signal(barrier, inc=1, device_id={"depth": lax.rem(me + hop, groups)},
                            device_id_type=pl.DeviceIdType.MESH)
    for target in (up, down):
        pl.semaphore_signal(barrier, inc=1, device_id={"tile": target}, device_id_type=pl.DeviceIdType.MESH)
    pl.semaphore_wait(barrier, groups + 1)

    @pl.loop(0, strips)
    def _(step):
        @pl.when(me < groups - 1)
        def _():
            front(strip_at(step, me + 1)[0]).start()

        @pl.when(me > 0)
        def _():
            back(strip_at(step, me - 1 + groups)[0]).start()

    zeros = jnp.zeros((rows, LANES), jnp.float32)

    if four:
        @pl.when(middle)
        def _():
            for k in range(own):
                for c in range(3):
                    got[me + 1, k, c] = zeros

    @pl.when(me == 0)
    def _():
        @pl.loop(0, strips)
        def _(strip):
            vol[0, strip + 1, body, :] = zeros

    @pl.when(me == groups - 1)
    def _():
        @pl.loop(0, strips)
        def _(strip):
            vol[slab + 1, strip + 1, body, :] = zeros

    @pl.loop(0, slab)
    def _(layer):
        vol[layer + 1, 0, body, :] = zeros
        vol[layer + 1, strips + 1, body, :] = zeros

    @pl.loop(0, strips)
    def _(strip):
        load(strip).wait()
        for layer in range(slab):
            top_out[strip, pl.ds(layer, 1), :] = vol[layer + 1, strip + 1, pl.ds(PAD, 1), :]
            bottom_out[strip, pl.ds(layer, 1), :] = vol[layer + 1, strip + 1, pl.ds(PAD + rows - 1, 1), :]

    @pl.when(tile < tiles - 1)
    def _():
        to_lower.start()

    @pl.when(tile > 0)
    def _():
        to_upper.start()

    @pl.when(tile == 0)
    def _():
        top_in[...] = jnp.zeros_like(top_in)

    @pl.when(tile == tiles - 1)
    def _():
        bottom_in[...] = jnp.zeros_like(bottom_in)

    @pl.when(tile > 0)
    def _():
        to_lower.wait_recv()

    @pl.when(tile < tiles - 1)
    def _():
        to_upper.wait_recv()

    @pl.loop(0, strips)
    def _(strip):
        for layer in range(slab):
            vol[layer + 1, strip + 1, pl.ds(PAD - 1, 1), :] = top_in[strip, pl.ds(layer, 1), :]
            vol[layer + 1, strip + 1, pl.ds(PAD + rows, 1), :] = bottom_in[strip, pl.ds(layer, 1), :]

    for copy in small:
        copy.wait()

    shape = (BLOCK, LANES)
    light_sq = light[0] * light[0] + light[1] * light[1] + light[2] * light[2]
    light_scale = 0.175 * lax.rsqrt(jnp.full(shape, light_sq, jnp.float32))
    light_z, light_x, light_y = (light[i] * light_scale for i in range(3))
    tone = [[0.5 * transfer[k, j] for j in range(3)] for k in range(3)]
    thick = [-LOG2E * transfer[3, j] for j in range(3)]
    lane = lax.broadcasted_iota(jnp.int32, shape, 1)
    first, last = lane == 0, lane == LANES - 1
    peak = 4.0 / depth_total

    @pl.loop(0, strips)
    def _(step):
        strip, target, k = strip_at(step, me)
        at = strip + 1

        @pl.when(me > 0)
        def _():
            front(strip).wait_recv()

        @pl.when(me < groups - 1)
        def _():
            back(strip).wait_recv()

        for low in range(0, rows, BLOCK):
            here = pl.ds(PAD + low, BLOCK)
            entered = entry[pl.ds(low, BLOCK), pl.ds(pl.multiple_of(strip * LANES, LANES), LANES)] - me * slab
            before, value = vol[0, at, here, :], vol[1, at, here, :]
            clear = jnp.ones(shape, jnp.float32)
            total = jnp.zeros(shape, jnp.float32)
            base = jnp.zeros(shape, jnp.float32)
            sums = [jnp.zeros(shape, jnp.float32)] * 3
            for layer in range(slab):
                after = vol[layer + 2, at, here, :]
                grad_z = after - before
                grad_x = vol[layer + 1, at, pl.ds(PAD + low + 1, BLOCK), :] - vol[
                    layer + 1, at, pl.ds(PAD + low - 1, BLOCK), :]
                right = jnp.where(first, vol[layer + 1, at + 1, here, :], value)
                left = jnp.where(last, vol[layer + 1, at - 1, here, :], value)
                grad_y = pltpu.roll(right, LANES - 1, 1) - pltpu.roll(left, 1, 1)
                square = 0.25 * (grad_z * grad_z + grad_x * grad_x + grad_y * grad_y) + 1.0
                inverse = lax.rsqrt(square)
                norm = square * inverse
                facing = jnp.abs(light_z * grad_z + light_x * grad_x + light_y * grad_y)
                half_shade = 0.15 + facing * inverse
                spread = 1.0 + jnp.exp2(jnp.minimum(thick[0] * value + thick[1] * norm + thick[2], 126.0))
                guess = pl.reciprocal(spread, approx=True)
                opacity = peak * (guess * (2.0 - spread * guess))
                opacity = jnp.where(entered <= layer, opacity, 0.0)
                weight = clear * opacity
                clear = clear - weight
                total = total + weight
                lit = weight * half_shade
                base = base + lit
                for c in range(3):
                    sums[c] = sums[c] + lit * jnp.tanh(tone[c][0] * value + tone[c][1] * norm + tone[c][2])
                before, value = value, after
            for c in range(3):
                sent[strip, c, pl.ds(low, BLOCK), :] = base + sums[c]
            sent[strip, 3, pl.ds(low, BLOCK), :] = total

        direct, passed, mid = route(target)

        @pl.when(direct)
        def _():
            piece(strip, target, me, k).start()

        if four:
            @pl.when(passed)
            def _():
                pass_in(strip, k).start()

            @pl.when(mid)
            def _():
                alpha_copy(k).start()

        @pl.when(target == me)
        def _():
            got[me, k] = sent[strip]

        if four:
            @pl.when(jnp.logical_and(jnp.logical_and(outer, target == diagonal), k > 0))
            def _():
                merge(k - 1)

    if four:
        @pl.when(outer)
        def _():
            merge(own - 1)

    for k in range(own):
        for hop in range(1, groups):
            source = lax.rem(me + hop, groups)
            if four:
                short = jnp.logical_and(middle, source == me + 1)

                @pl.when(short)
                def _():
                    later_copy(k, me).wait_recv()

                @pl.when(jnp.logical_not(short))
                def _():
                    piece(source * own + k, source, source, k).wait_recv()
            else:
                piece(source * own + k, source, source, k).wait_recv()
        for low in range(0, rows, BLOCK):
            here = pl.ds(low, BLOCK)
            clear = jnp.ones(shape, jnp.float32)
            sums = [jnp.zeros(shape, jnp.float32)] * 4
            for source in range(groups):
                alpha = got[source, k, 3, here, :]
                for c in range(3):
                    sums[c] = sums[c] + clear * got[source, k, c, here, :]
                sums[3] = sums[3] + clear * alpha
                clear = clear - clear * alpha
            for c in range(4):
                out[c, here, pl.ds(k * LANES, LANES)] = sums[c]

    @pl.loop(0, strips)
    def _(step):
        strip, target, k = strip_at(step, me)

        @pl.when(me < groups - 1)
        def _():
            front(strip).wait_send()

        @pl.when(me > 0)
        def _():
            back(strip).wait_send()

        direct, passed, mid = route(target)

        @pl.when(direct)
        def _():
            piece(strip, target, me, k).wait_send()

        if four:
            @pl.when(passed)
            def _():
                pass_in(strip, k).wait_send()

            @pl.when(mid)
            def _():
                alpha_copy(k).wait_send()

    if four:
        @pl.when(outer)
        def _():
            for k in range(own):
                merged_copy(k, mate).wait_send()
                later_copy(k, mate).wait_send()

    @pl.when(tile < tiles - 1)
    def _():
        to_lower.wait_send()

    @pl.when(tile > 0)
    def _():
        to_upper.wait_send()


def local(volume, entry_depth, light_dir, transfer):
    slab, rows, columns = volume.shape
    groups, tiles = lax.axis_size("depth"), lax.axis_size("tile")
    strips = columns // LANES
    own = strips // groups
    edge = pltpu.VMEM((strips, slab, LANES), jnp.float32)
    return pl.pallas_call(
        functools.partial(kernel, groups, tiles, float(slab * groups)),
        out_shape=jax.ShapeDtypeStruct((4, rows, columns // groups), jnp.float32),
        in_specs=[pl.BlockSpec(memory_space=pl.ANY)] * 4,
        out_specs=pl.BlockSpec(memory_space=pltpu.VMEM),
        scratch_shapes=[
            pltpu.VMEM((rows, columns), jnp.int32),
            pltpu.SMEM((3,), jnp.float32),
            pltpu.SMEM((4, 3), jnp.float32),
            pltpu.VMEM((slab + 2, strips + 2, rows + 2 * PAD, LANES), jnp.float32),
            edge,
            edge,
            edge,
            edge,
            pltpu.VMEM((strips, 4, rows, LANES), jnp.float32),
            pltpu.VMEM((groups, own, 4, rows, LANES), jnp.float32),
            pltpu.VMEM((own, 4, rows, LANES), jnp.float32),
            pltpu.VMEM((own, rows, LANES), jnp.float32),
            pltpu.VMEM((own, 5, rows, LANES), jnp.float32),
            pltpu.SemaphoreType.DMA((3,)),
            pltpu.SemaphoreType.DMA((strips,)),
            pltpu.SemaphoreType.DMA((2, strips)),
            pltpu.SemaphoreType.DMA((2, strips)),
            pltpu.SemaphoreType.DMA((2, 2)),
            pltpu.SemaphoreType.DMA((strips,)),
            pltpu.SemaphoreType.DMA((groups, own)),
            pltpu.SemaphoreType.DMA((own,)),
            pltpu.SemaphoreType.DMA((2, own)),
            pltpu.SemaphoreType.DMA((2, own)),
        ],
        compiler_params=pltpu.CompilerParams(
            collective_id=0, has_side_effects=True, vmem_limit_bytes=60 * 1024 * 1024
        ),
        cost_estimate=pl.CostEstimate(
            flops=60 * slab * rows * columns, bytes_accessed=4 * slab * rows * columns, transcendentals=6 * slab * rows * columns
        ),
    )(volume, entry_depth, light_dir, transfer)


def solution(mesh):
    placed = (P("depth", "tile", None), P("tile", None), P(), P())
    return jax.shard_map(
        local, mesh=mesh, in_specs=placed, out_specs=P(None, "tile", "depth"), check_vma=False
    )
```

```python
import functools
import math

import jax
import jax.numpy as jnp
from jax import lax
from jax.experimental import pallas as pl
from jax.experimental.pallas import tpu as pltpu
from jax.sharding import PartitionSpec as P

LANES = 128
PAD = 8
BLOCK = 16
LOG2E = 1.4426950408889634


def kernel(groups, tiles, depth_total, volume, entry_hbm, light_hbm, transfer_hbm, out, entry, light, transfer, vol, top_out, bottom_out, top_in,
           bottom_in, sent, got, passing, small_sem, load_sem, front_sem, back_sem, row_sem, piece_send, piece_recv, pass_send, pass_recv):
    slab, rows, columns = volume.shape
    strips = columns // LANES
    own = strips // groups
    me, tile = lax.axis_index("depth"), lax.axis_index("tile")
    body = pl.ds(PAD, rows)

    def load(strip):
        return pltpu.make_async_copy(
            volume.at[:, :, pl.ds(pl.multiple_of(strip * LANES, LANES), LANES)],
            vol.at[pl.ds(1, slab), strip + 1, body, :],
            load_sem.at[strip],
        )

    def front(strip):
        return pltpu.make_async_remote_copy(
            src_ref=volume.at[slab - 1, :, pl.ds(pl.multiple_of(strip * LANES, LANES), LANES)],
            dst_ref=vol.at[0, strip + 1, body, :],
            send_sem=front_sem.at[0, strip],
            recv_sem=front_sem.at[1, strip],
            device_id={"depth": lax.rem(me + 1, groups)},
            device_id_type=pl.DeviceIdType.MESH,
        )

    def back(strip):
        return pltpu.make_async_remote_copy(
            src_ref=volume.at[0, :, pl.ds(pl.multiple_of(strip * LANES, LANES), LANES)],
            dst_ref=vol.at[slab + 1, strip + 1, body, :],
            send_sem=back_sem.at[0, strip],
            recv_sem=back_sem.at[1, strip],
            device_id={"depth": lax.rem(me + groups - 1, groups)},
            device_id_type=pl.DeviceIdType.MESH,
        )

    def row_copy(src, dst, way, target):
        return pltpu.make_async_remote_copy(
            src_ref=src,
            dst_ref=dst,
            send_sem=row_sem.at[0, way],
            recv_sem=row_sem.at[1, way],
            device_id={"tile": target},
            device_id_type=pl.DeviceIdType.MESH,
        )

    def piece(strip, target, source, k):
        return pltpu.make_async_remote_copy(
            src_ref=sent.at[strip],
            dst_ref=got.at[source, k],
            send_sem=piece_send.at[strip],
            recv_sem=piece_recv.at[source, k],
            device_id={"depth": target},
            device_id_type=pl.DeviceIdType.MESH,
        )

    relays = own // 2 if groups == 4 else 0
    middle = jnp.logical_and(me > 0, me < groups - 1)

    def pass_in(strip, k):
        return pltpu.make_async_remote_copy(
            src_ref=sent.at[strip],
            dst_ref=passing.at[k],
            send_sem=piece_send.at[strip],
            recv_sem=pass_recv.at[k],
            device_id={"depth": lax.rem(me + 2, groups)},
            device_id_type=pl.DeviceIdType.MESH,
        )

    def pass_on(k):
        target = jnp.where(me == 0, 1, 2)
        source = 3 - target
        return pltpu.make_async_remote_copy(
            src_ref=passing.at[k],
            dst_ref=got.at[source, k],
            send_sem=pass_send.at[k],
            recv_sem=piece_recv.at[source, k],
            device_id={"depth": target},
            device_id_type=pl.DeviceIdType.MESH,
        )

    def strip_at(step, device):
        others = groups - 1
        away = step < own * others
        k = jnp.where(away, step // others, step - own * others)
        target = lax.rem(device + jnp.where(away, 1 + lax.rem(step, others), 0), groups)
        return target * own + k, target, k

    up, down = lax.rem(tile + tiles - 1, tiles), lax.rem(tile + 1, tiles)
    to_lower = row_copy(bottom_out, top_in, 0, down)
    to_upper = row_copy(top_out, bottom_in, 1, up)

    small = [
        pltpu.make_async_copy(src, dst, small_sem.at[i])
        for i, (src, dst) in enumerate(((entry_hbm, entry), (light_hbm, light), (transfer_hbm, transfer)))
    ]

    @pl.loop(0, strips)
    def _(strip):
        load(strip).start()

    for copy in small:
        copy.start()

    barrier = pltpu.get_barrier_semaphore()
    for hop in range(1, groups):
        pl.semaphore_signal(barrier, inc=1, device_id={"depth": lax.rem(me + hop, groups)},
                            device_id_type=pl.DeviceIdType.MESH)
    for target in (up, down):
        pl.semaphore_signal(barrier, inc=1, device_id={"tile": target}, device_id_type=pl.DeviceIdType.MESH)
    pl.semaphore_wait(barrier, groups + 1)

    @pl.loop(0, strips)
    def _(step):
        @pl.when(me < groups - 1)
        def _():
            front(strip_at(step, me + 1)[0]).start()

        @pl.when(me > 0)
        def _():
            back(strip_at(step, me - 1 + groups)[0]).start()

    zeros = jnp.zeros((rows, LANES), jnp.float32)

    @pl.when(me == 0)
    def _():
        @pl.loop(0, strips)
        def _(strip):
            vol[0, strip + 1, body, :] = zeros

    @pl.when(me == groups - 1)
    def _():
        @pl.loop(0, strips)
        def _(strip):
            vol[slab + 1, strip + 1, body, :] = zeros

    @pl.loop(0, slab)
    def _(layer):
        vol[layer + 1, 0, body, :] = zeros
        vol[layer + 1, strips + 1, body, :] = zeros

    @pl.loop(0, strips)
    def _(strip):
        load(strip).wait()
        for layer in range(slab):
            top_out[strip, pl.ds(layer, 1), :] = vol[layer + 1, strip + 1, pl.ds(PAD, 1), :]
            bottom_out[strip, pl.ds(layer, 1), :] = vol[layer + 1, strip + 1, pl.ds(PAD + rows - 1, 1), :]

    @pl.when(tile < tiles - 1)
    def _():
        to_lower.start()

    @pl.when(tile > 0)
    def _():
        to_upper.start()

    @pl.when(tile == 0)
    def _():
        top_in[...] = jnp.zeros_like(top_in)

    @pl.when(tile == tiles - 1)
    def _():
        bottom_in[...] = jnp.zeros_like(bottom_in)

    @pl.when(tile > 0)
    def _():
        to_lower.wait_recv()

    @pl.when(tile < tiles - 1)
    def _():
        to_upper.wait_recv()

    @pl.loop(0, strips)
    def _(strip):
        for layer in range(slab):
            vol[layer + 1, strip + 1, pl.ds(PAD - 1, 1), :] = top_in[strip, pl.ds(layer, 1), :]
            vol[layer + 1, strip + 1, pl.ds(PAD + rows, 1), :] = bottom_in[strip, pl.ds(layer, 1), :]

    for copy in small:
        copy.wait()

    shape = (BLOCK, LANES)
    light_sq = light[0] * light[0] + light[1] * light[1] + light[2] * light[2]
    light_scale = 0.35 * lax.rsqrt(jnp.full(shape, light_sq, jnp.float32))
    light_z, light_x, light_y = (light[i] * light_scale for i in range(3))
    halves = (0.5, 0.25, 0.5)
    tone = [[halves[j] * transfer[k, j] for j in range(3)] for k in range(3)]
    peak = 4.0 / depth_total
    thick = [-LOG2E * transfer[3, 0], -0.5 * LOG2E * transfer[3, 1], -LOG2E * transfer[3, 2] - math.log2(peak)]
    lane = lax.broadcasted_iota(jnp.int32, shape, 1)
    first, last = lane == 0, lane == LANES - 1

    @pl.loop(0, strips)
    def _(step):
        strip, target, k = strip_at(step, me)
        at = strip + 1

        @pl.when(me > 0)
        def _():
            front(strip).wait_recv()

        @pl.when(me < groups - 1)
        def _():
            back(strip).wait_recv()

        for low in range(0, rows, BLOCK):
            here = pl.ds(PAD + low, BLOCK)
            entered = entry[pl.ds(low, BLOCK), pl.ds(pl.multiple_of(strip * LANES, LANES), LANES)] - me * slab
            before, value = vol[0, at, here, :], vol[1, at, here, :]
            clear = jnp.ones(shape, jnp.float32)
            total = jnp.zeros(shape, jnp.float32)
            base = jnp.zeros(shape, jnp.float32)
            sums = [jnp.zeros(shape, jnp.float32)] * 3
            for layer in range(slab):
                after = vol[layer + 2, at, here, :]
                grad_z = after - before
                grad_x = vol[layer + 1, at, pl.ds(PAD + low + 1, BLOCK), :] - vol[
                    layer + 1, at, pl.ds(PAD + low - 1, BLOCK), :]
                right = jnp.where(first, vol[layer + 1, at + 1, here, :], value)
                left = jnp.where(last, vol[layer + 1, at - 1, here, :], value)
                grad_y = pltpu.roll(right, LANES - 1, 1) - pltpu.roll(left, 1, 1)
                square = (grad_z * grad_z + grad_x * grad_x) + (grad_y * grad_y + 4.0)
                inverse = lax.rsqrt(square)
                norm = square * inverse
                facing = jnp.abs(light_z * grad_z + light_x * grad_x + light_y * grad_y)
                half_shade = 0.15 + facing * inverse
                spread = 1.0 / peak + jnp.exp2(jnp.minimum(thick[0] * value + thick[1] * norm + thick[2], 126.0))
                guess = pl.reciprocal(spread, approx=True)
                opacity = guess * (2.0 - spread * guess)
                opacity = jnp.where(entered <= layer, opacity, 0.0)
                weight = clear * opacity
                clear = clear - weight
                total = total + weight
                lit = weight * half_shade
                base = base + lit
                for c in range(3):
                    sums[c] = sums[c] + lit * jnp.tanh(tone[c][0] * value + tone[c][1] * norm + tone[c][2])
                before, value = value, after
            for c in range(3):
                sent[strip, c, pl.ds(low, BLOCK), :] = base + sums[c]
            sent[strip, 3, pl.ds(low, BLOCK), :] = total

        relayed = jnp.logical_and(jnp.logical_and(middle, target == 3 - me), k < relays)

        @pl.when(jnp.logical_and(target != me, jnp.logical_not(relayed)))
        def _():
            piece(strip, target, me, k).start()

        if relays:
            @pl.when(relayed)
            def _():
                pass_in(strip, k).start()

            @pl.when(jnp.logical_and(jnp.logical_not(middle), jnp.logical_and(target == lax.rem(me + 1, groups), k >= own - relays)))
            def _():
                pass_in(strip, k - (own - relays)).wait_recv()
                pass_on(k - (own - relays)).start()

        @pl.when(target == me)
        def _():
            got[me, k] = sent[strip]

    for k in range(own):
        for hop in range(1, groups):
            source = lax.rem(me + hop, groups)
            piece(source * own + k, source, source, k).wait_recv()
        for low in range(0, rows, BLOCK):
            here = pl.ds(low, BLOCK)
            clear = jnp.ones(shape, jnp.float32)
            sums = [jnp.zeros(shape, jnp.float32)] * 4
            for source in range(groups):
                alpha = got[source, k, 3, here, :]
                for c in range(3):
                    sums[c] = sums[c] + clear * got[source, k, c, here, :]
                sums[3] = sums[3] + clear * alpha
                clear = clear - clear * alpha
            for c in range(4):
                out[c, here, pl.ds(k * LANES, LANES)] = sums[c]

    @pl.loop(0, strips)
    def _(step):
        strip, target, k = strip_at(step, me)

        @pl.when(me < groups - 1)
        def _():
            front(strip).wait_send()

        @pl.when(me > 0)
        def _():
            back(strip).wait_send()

        @pl.when(target != me)
        def _():
            piece(strip, target, me, k).wait_send()

    if relays:
        @pl.when(jnp.logical_not(middle))
        def _():
            for k in range(relays):
                pass_on(k).wait_send()

    @pl.when(tile < tiles - 1)
    def _():
        to_lower.wait_send()

    @pl.when(tile > 0)
    def _():
        to_upper.wait_send()


def local(volume, entry_depth, light_dir, transfer):
    slab, rows, columns = volume.shape
    groups, tiles = lax.axis_size("depth"), lax.axis_size("tile")
    strips = columns // LANES
    own = strips // groups
    edge = pltpu.VMEM((strips, slab, LANES), jnp.float32)
    return pl.pallas_call(
        functools.partial(kernel, groups, tiles, float(slab * groups)),
        out_shape=jax.ShapeDtypeStruct((4, rows, columns // groups), jnp.float32),
        in_specs=[pl.BlockSpec(memory_space=pl.ANY)] * 4,
        out_specs=pl.BlockSpec(memory_space=pltpu.VMEM),
        scratch_shapes=[
            pltpu.VMEM((rows, columns), jnp.int32),
            pltpu.SMEM((3,), jnp.float32),
            pltpu.SMEM((4, 3), jnp.float32),
            pltpu.VMEM((slab + 2, strips + 2, rows + 2 * PAD, LANES), jnp.float32),
            edge,
            edge,
            edge,
            edge,
            pltpu.VMEM((strips, 4, rows, LANES), jnp.float32),
            pltpu.VMEM((groups, own, 4, rows, LANES), jnp.float32),
            pltpu.VMEM((max(own // 2, 1), 4, rows, LANES), jnp.float32),
            pltpu.SemaphoreType.DMA((3,)),
            pltpu.SemaphoreType.DMA((strips,)),
            pltpu.SemaphoreType.DMA((2, strips)),
            pltpu.SemaphoreType.DMA((2, strips)),
            pltpu.SemaphoreType.DMA((2, 2)),
            pltpu.SemaphoreType.DMA((strips,)),
            pltpu.SemaphoreType.DMA((groups, own)),
            pltpu.SemaphoreType.DMA((max(own // 2, 1),)),
            pltpu.SemaphoreType.DMA((max(own // 2, 1),)),
        ],
        compiler_params=pltpu.CompilerParams(
            collective_id=0, has_side_effects=True, vmem_limit_bytes=60 * 1024 * 1024
        ),
        cost_estimate=pl.CostEstimate(
            flops=60 * slab * rows * columns, bytes_accessed=4 * slab * rows * columns, transcendentals=6 * slab * rows * columns
        ),
    )(volume, entry_depth, light_dir, transfer)


def solution(mesh):
    placed = (P("depth", "tile", None), P("tile", None), P(), P())
    return jax.shard_map(
        local, mesh=mesh, in_specs=placed, out_specs=P(None, "tile", "depth"), check_vma=False
    )
```

```python
import functools
import math

import jax
import jax.numpy as jnp
from jax import lax
from jax.experimental import pallas as pl
from jax.experimental.pallas import tpu as pltpu
from jax.sharding import PartitionSpec as P

LANES = 128
PAD = 8
BLOCK = 16
LOG2E = 1.4426950408889634


def kernel(groups, tiles, depth_total, volume, entry_hbm, light_hbm, transfer_hbm, out, entry, light, transfer, vol, top_out, bottom_out, top_in,
           bottom_in, sent, got, passing, between, merged, small_sem, load_sem, front_sem, back_sem, row_sem, piece_send, piece_recv, pass_recv, alpha_sem, merged_sem):
    slab, rows, columns = volume.shape
    strips = columns // LANES
    own = strips // groups
    me, tile = lax.axis_index("depth"), lax.axis_index("tile")
    body = pl.ds(PAD, rows)

    def load(strip):
        return pltpu.make_async_copy(
            volume.at[:, :, pl.ds(pl.multiple_of(strip * LANES, LANES), LANES)],
            vol.at[pl.ds(1, slab), strip + 1, body, :],
            load_sem.at[strip],
        )

    def front(strip):
        return pltpu.make_async_remote_copy(
            src_ref=volume.at[slab - 1, :, pl.ds(pl.multiple_of(strip * LANES, LANES), LANES)],
            dst_ref=vol.at[0, strip + 1, body, :],
            send_sem=front_sem.at[0, strip],
            recv_sem=front_sem.at[1, strip],
            device_id={"depth": lax.rem(me + 1, groups)},
            device_id_type=pl.DeviceIdType.MESH,
        )

    def back(strip):
        return pltpu.make_async_remote_copy(
            src_ref=volume.at[0, :, pl.ds(pl.multiple_of(strip * LANES, LANES), LANES)],
            dst_ref=vol.at[slab + 1, strip + 1, body, :],
            send_sem=back_sem.at[0, strip],
            recv_sem=back_sem.at[1, strip],
            device_id={"depth": lax.rem(me + groups - 1, groups)},
            device_id_type=pl.DeviceIdType.MESH,
        )

    def row_copy(src, dst, way, target):
        return pltpu.make_async_remote_copy(
            src_ref=src,
            dst_ref=dst,
            send_sem=row_sem.at[0, way],
            recv_sem=row_sem.at[1, way],
            device_id={"tile": target},
            device_id_type=pl.DeviceIdType.MESH,
        )

    def piece(strip, target, source, k):
        return pltpu.make_async_remote_copy(
            src_ref=sent.at[strip],
            dst_ref=got.at[source, k],
            send_sem=piece_send.at[strip],
            recv_sem=piece_recv.at[source, k],
            device_id={"depth": target},
            device_id_type=pl.DeviceIdType.MESH,
        )

    four = groups == 4
    mate, across, diagonal = me + 1 - 2 * lax.rem(me, 2), lax.rem(me + 2, groups), 3 - me
    middle = jnp.logical_and(me > 0, me < groups - 1)
    outer = jnp.logical_not(middle)

    def pass_in(strip, k):
        return pltpu.make_async_remote_copy(
            src_ref=sent.at[strip],
            dst_ref=passing.at[k],
            send_sem=piece_send.at[strip],
            recv_sem=pass_recv.at[k],
            device_id={"depth": across},
            device_id_type=pl.DeviceIdType.MESH,
        )

    def alpha_copy(k):
        return pltpu.make_async_remote_copy(
            src_ref=sent.at[me * own + k, 3],
            dst_ref=between.at[k],
            send_sem=alpha_sem.at[0, k],
            recv_sem=alpha_sem.at[1, k],
            device_id={"depth": mate},
            device_id_type=pl.DeviceIdType.MESH,
        )

    def merged_copy(k, target):
        return pltpu.make_async_remote_copy(
            src_ref=merged.at[k, pl.ds(0, 4)],
            dst_ref=got.at[target - 1, k],
            send_sem=merged_sem.at[0, k],
            recv_sem=piece_recv.at[target - 1, k],
            device_id={"depth": target},
            device_id_type=pl.DeviceIdType.MESH,
        )

    def later_copy(k, target):
        return pltpu.make_async_remote_copy(
            src_ref=merged.at[k, pl.ds(4, 1)],
            dst_ref=got.at[target + 1, k, pl.ds(3, 1)],
            send_sem=merged_sem.at[1, k],
            recv_sem=piece_recv.at[target + 1, k],
            device_id={"depth": target},
            device_id_type=pl.DeviceIdType.MESH,
        )

    def merge(k):
        pass_in(mate * own + k, k).wait_recv()
        alpha_copy(k).wait_recv()

        def combine(front_part, back_part):
            for low in range(0, rows, BLOCK):
                here = pl.ds(low, BLOCK)
                alpha = front_part[3, here, :]
                clear = (1.0 - alpha) * (1.0 - between[k, here, :])
                for c in range(3):
                    merged[k, c, here, :] = front_part[c, here, :] + clear * back_part[c, here, :]
                merged[k, 3, here, :] = alpha
                merged[k, 4, here, :] = back_part[3, here, :]

        @pl.when(me == 0)
        def _():
            combine(sent.at[mate * own + k], passing.at[k])

        @pl.when(me != 0)
        def _():
            combine(passing.at[k], sent.at[mate * own + k])

        merged_copy(k, mate).start()
        later_copy(k, mate).start()

    def route(target):
        if not four:
            no = target != target
            return target != me, no, no
        passed = jnp.logical_and(middle, target == diagonal)
        kept = jnp.logical_and(outer, target == mate)
        direct = jnp.logical_and(target != me, jnp.logical_not(jnp.logical_or(passed, kept)))
        return direct, passed, jnp.logical_and(middle, target == me)

    def strip_at(step, device):
        if four:
            device = lax.rem(device, groups)
            beside = device + 1 - 2 * lax.rem(device, 2)
            opposite = lax.rem(device + 2, groups)
            inner = jnp.logical_and(device > 0, device < groups - 1)
            section, early = step // own, jnp.logical_and(inner, step < 2 * own)
            k = jnp.where(early, step // 2, lax.rem(step, own))
            outer_target = jnp.where(
                section == 0,
                3 - device,
                jnp.where(section == 1, beside, jnp.where(section == 2, opposite, device)),
            )
            inner_target = jnp.where(
                early,
                jnp.where(lax.rem(step, 2) == 0, 3 - device, device),
                jnp.where(section == 2, beside, opposite),
            )
            target = jnp.where(inner, inner_target, outer_target)
        else:
            k, turn = step // groups, lax.rem(step, groups)
            target = lax.rem(device + 1 + turn, groups)
        return target * own + k, target, k

    up, down = lax.rem(tile + tiles - 1, tiles), lax.rem(tile + 1, tiles)
    to_lower = row_copy(bottom_out, top_in, 0, down)
    to_upper = row_copy(top_out, bottom_in, 1, up)

    small = [
        pltpu.make_async_copy(src, dst, small_sem.at[i])
        for i, (src, dst) in enumerate(((entry_hbm, entry), (light_hbm, light), (transfer_hbm, transfer)))
    ]

    @pl.loop(0, strips)
    def _(strip):
        load(strip).start()

    for copy in small:
        copy.start()

    barrier = pltpu.get_barrier_semaphore()
    for hop in range(1, groups):
        pl.semaphore_signal(barrier, inc=1, device_id={"depth": lax.rem(me + hop, groups)},
                            device_id_type=pl.DeviceIdType.MESH)
    for target in (up, down):
        pl.semaphore_signal(barrier, inc=1, device_id={"tile": target}, device_id_type=pl.DeviceIdType.MESH)
    pl.semaphore_wait(barrier, groups + 1)

    @pl.loop(0, strips)
    def _(step):
        @pl.when(me < groups - 1)
        def _():
            front(strip_at(step, me + 1)[0]).start()

        @pl.when(me > 0)
        def _():
            back(strip_at(step, me - 1 + groups)[0]).start()

    zeros = jnp.zeros((rows, LANES), jnp.float32)

    if four:
        @pl.when(middle)
        def _():
            for k in range(own):
                for c in range(3):
                    got[me + 1, k, c] = zeros

    @pl.when(me == 0)
    def _():
        @pl.loop(0, strips)
        def _(strip):
            vol[0, strip + 1, body, :] = zeros

    @pl.when(me == groups - 1)
    def _():
        @pl.loop(0, strips)
        def _(strip):
            vol[slab + 1, strip + 1, body, :] = zeros

    @pl.loop(0, slab)
    def _(layer):
        vol[layer + 1, 0, body, :] = zeros
        vol[layer + 1, strips + 1, body, :] = zeros

    @pl.loop(0, strips)
    def _(strip):
        load(strip).wait()
        for layer in range(slab):
            top_out[strip, pl.ds(layer, 1), :] = vol[layer + 1, strip + 1, pl.ds(PAD, 1), :]
            bottom_out[strip, pl.ds(layer, 1), :] = vol[layer + 1, strip + 1, pl.ds(PAD + rows - 1, 1), :]

    @pl.when(tile < tiles - 1)
    def _():
        to_lower.start()

    @pl.when(tile > 0)
    def _():
        to_upper.start()

    @pl.when(tile == 0)
    def _():
        top_in[...] = jnp.zeros_like(top_in)

    @pl.when(tile == tiles - 1)
    def _():
        bottom_in[...] = jnp.zeros_like(bottom_in)

    @pl.when(tile > 0)
    def _():
        to_lower.wait_recv()

    @pl.when(tile < tiles - 1)
    def _():
        to_upper.wait_recv()

    @pl.loop(0, strips)
    def _(strip):
        for layer in range(slab):
            vol[layer + 1, strip + 1, pl.ds(PAD - 1, 1), :] = top_in[strip, pl.ds(layer, 1), :]
            vol[layer + 1, strip + 1, pl.ds(PAD + rows, 1), :] = bottom_in[strip, pl.ds(layer, 1), :]

    for copy in small:
        copy.wait()

    shape = (BLOCK, LANES)
    light_sq = light[0] * light[0] + light[1] * light[1] + light[2] * light[2]
    light_scale = 0.35 * lax.rsqrt(jnp.full(shape, light_sq, jnp.float32))
    light_z, light_x, light_y = (light[i] * light_scale for i in range(3))
    halves = (0.5, 0.25, 0.5)
    tone = [[halves[j] * transfer[k, j] for j in range(3)] for k in range(3)]
    peak = 4.0 / depth_total
    thick = [-LOG2E * transfer[3, 0], -0.5 * LOG2E * transfer[3, 1], -LOG2E * transfer[3, 2] - math.log2(peak)]
    lane = lax.broadcasted_iota(jnp.int32, shape, 1)
    first, last = lane == 0, lane == LANES - 1

    @pl.loop(0, strips)
    def _(step):
        strip, target, k = strip_at(step, me)
        at = strip + 1

        @pl.when(me > 0)
        def _():
            front(strip).wait_recv()

        @pl.when(me < groups - 1)
        def _():
            back(strip).wait_recv()

        for low in range(0, rows, BLOCK):
            here = pl.ds(PAD + low, BLOCK)
            entered = entry[pl.ds(low, BLOCK), pl.ds(pl.multiple_of(strip * LANES, LANES), LANES)] - me * slab
            before, value = vol[0, at, here, :], vol[1, at, here, :]
            clear = jnp.ones(shape, jnp.float32)
            total = jnp.zeros(shape, jnp.float32)
            base = jnp.zeros(shape, jnp.float32)
            sums = [jnp.zeros(shape, jnp.float32)] * 3
            for layer in range(slab):
                after = vol[layer + 2, at, here, :]
                grad_z = after - before
                grad_x = vol[layer + 1, at, pl.ds(PAD + low + 1, BLOCK), :] - vol[
                    layer + 1, at, pl.ds(PAD + low - 1, BLOCK), :]
                right = jnp.where(first, vol[layer + 1, at + 1, here, :], value)
                left = jnp.where(last, vol[layer + 1, at - 1, here, :], value)
                grad_y = pltpu.roll(right, LANES - 1, 1) - pltpu.roll(left, 1, 1)
                square = (grad_z * grad_z + grad_x * grad_x) + (grad_y * grad_y + 4.0)
                inverse = lax.rsqrt(square)
                norm = square * inverse
                facing = jnp.abs(light_z * grad_z + light_x * grad_x + light_y * grad_y)
                half_shade = 0.15 + facing * inverse
                spread = 1.0 / peak + jnp.exp2(jnp.minimum(thick[0] * value + thick[1] * norm + thick[2], 126.0))
                guess = pl.reciprocal(spread, approx=True)
                opacity = guess * (2.0 - spread * guess)
                opacity = jnp.where(entered <= layer, opacity, 0.0)
                weight = clear * opacity
                clear = clear - weight
                total = total + weight
                lit = weight * half_shade
                base = base + lit
                for c in range(3):
                    sums[c] = sums[c] + lit * jnp.tanh(tone[c][0] * value + tone[c][1] * norm + tone[c][2])
                before, value = value, after
            for c in range(3):
                sent[strip, c, pl.ds(low, BLOCK), :] = base + sums[c]
            sent[strip, 3, pl.ds(low, BLOCK), :] = total

        direct, passed, mid = route(target)

        @pl.when(direct)
        def _():
            piece(strip, target, me, k).start()

        if four:
            @pl.when(passed)
            def _():
                pass_in(strip, k).start()

            @pl.when(mid)
            def _():
                alpha_copy(k).start()

        @pl.when(target == me)
        def _():
            got[me, k] = sent[strip]

        if four:
            @pl.when(jnp.logical_and(outer, jnp.logical_and(step > 2 * own, step <= 3 * own)))
            def _():
                merge(step - (2 * own + 1))

    for k in range(own):
        for hop in range(1, groups):
            source = lax.rem(me + hop, groups)
            if four:
                short = jnp.logical_and(middle, source == me + 1)

                @pl.when(short)
                def _():
                    later_copy(k, me).wait_recv()

                @pl.when(jnp.logical_not(short))
                def _():
                    piece(source * own + k, source, source, k).wait_recv()
            else:
                piece(source * own + k, source, source, k).wait_recv()
        for low in range(0, rows, BLOCK):
            here = pl.ds(low, BLOCK)
            clear = jnp.ones(shape, jnp.float32)
            sums = [jnp.zeros(shape, jnp.float32)] * 4
            for source in range(groups):
                alpha = got[source, k, 3, here, :]
                for c in range(3):
                    sums[c] = sums[c] + clear * got[source, k, c, here, :]
                sums[3] = sums[3] + clear * alpha
                clear = clear - clear * alpha
            for c in range(4):
                out[c, here, pl.ds(k * LANES, LANES)] = sums[c]

    @pl.loop(0, strips)
    def _(step):
        strip, target, k = strip_at(step, me)

        @pl.when(me < groups - 1)
        def _():
            front(strip).wait_send()

        @pl.when(me > 0)
        def _():
            back(strip).wait_send()

        direct, passed, mid = route(target)

        @pl.when(direct)
        def _():
            piece(strip, target, me, k).wait_send()

        if four:
            @pl.when(passed)
            def _():
                pass_in(strip, k).wait_send()

            @pl.when(mid)
            def _():
                alpha_copy(k).wait_send()

    if four:
        @pl.when(outer)
        def _():
            for k in range(own):
                merged_copy(k, mate).wait_send()
                later_copy(k, mate).wait_send()

    @pl.when(tile < tiles - 1)
    def _():
        to_lower.wait_send()

    @pl.when(tile > 0)
    def _():
        to_upper.wait_send()


def local(volume, entry_depth, light_dir, transfer):
    slab, rows, columns = volume.shape
    groups, tiles = lax.axis_size("depth"), lax.axis_size("tile")
    strips = columns // LANES
    own = strips // groups
    edge = pltpu.VMEM((strips, slab, LANES), jnp.float32)
    return pl.pallas_call(
        functools.partial(kernel, groups, tiles, float(slab * groups)),
        out_shape=jax.ShapeDtypeStruct((4, rows, columns // groups), jnp.float32),
        in_specs=[pl.BlockSpec(memory_space=pl.ANY)] * 4,
        out_specs=pl.BlockSpec(memory_space=pltpu.VMEM),
        scratch_shapes=[
            pltpu.VMEM((rows, columns), jnp.int32),
            pltpu.SMEM((3,), jnp.float32),
            pltpu.SMEM((4, 3), jnp.float32),
            pltpu.VMEM((slab + 2, strips + 2, rows + 2 * PAD, LANES), jnp.float32),
            edge,
            edge,
            edge,
            edge,
            pltpu.VMEM((strips, 4, rows, LANES), jnp.float32),
            pltpu.VMEM((groups, own, 4, rows, LANES), jnp.float32),
            pltpu.VMEM((own, 4, rows, LANES), jnp.float32),
            pltpu.VMEM((own, rows, LANES), jnp.float32),
            pltpu.VMEM((own, 5, rows, LANES), jnp.float32),
            pltpu.SemaphoreType.DMA((3,)),
            pltpu.SemaphoreType.DMA((strips,)),
            pltpu.SemaphoreType.DMA((2, strips)),
            pltpu.SemaphoreType.DMA((2, strips)),
            pltpu.SemaphoreType.DMA((2, 2)),
            pltpu.SemaphoreType.DMA((strips,)),
            pltpu.SemaphoreType.DMA((groups, own)),
            pltpu.SemaphoreType.DMA((own,)),
            pltpu.SemaphoreType.DMA((2, own)),
            pltpu.SemaphoreType.DMA((2, own)),
        ],
        compiler_params=pltpu.CompilerParams(
            collective_id=0, has_side_effects=True, vmem_limit_bytes=60 * 1024 * 1024
        ),
        cost_estimate=pl.CostEstimate(
            flops=60 * slab * rows * columns, bytes_accessed=4 * slab * rows * columns, transcendentals=6 * slab * rows * columns
        ),
    )(volume, entry_depth, light_dir, transfer)


def solution(mesh):
    placed = (P("depth", "tile", None), P("tile", None), P(), P())
    return jax.shard_map(
        local, mesh=mesh, in_specs=placed, out_specs=P(None, "tile", "depth"), check_vma=False
    )
```

```python
import functools
import math

import jax
import jax.numpy as jnp
from jax import lax
from jax.experimental import pallas as pl
from jax.experimental.pallas import tpu as pltpu
from jax.sharding import PartitionSpec as P

LANES = 128
PAD = 8
BLOCK = 16
LOG2E = 1.4426950408889634


def kernel(groups, tiles, depth_total, volume, entry_hbm, light_hbm, transfer_hbm, got, entry, light, transfer, vol, top_out, bottom_out, top_in,
           bottom_in, sent, passing, small_sem, load_sem, front_sem, back_sem, row_sem, piece_send, piece_recv, pass_send, pass_recv, own_sem):
    slab, rows, columns = volume.shape
    strips = columns // LANES
    own = strips // groups
    me, tile = lax.axis_index("depth"), lax.axis_index("tile")
    body = pl.ds(PAD, rows)

    def load(strip):
        return pltpu.make_async_copy(
            volume.at[:, :, pl.ds(pl.multiple_of(strip * LANES, LANES), LANES)],
            vol.at[pl.ds(1, slab), strip + 1, body, :],
            load_sem.at[strip],
        )

    def front(strip):
        return pltpu.make_async_remote_copy(
            src_ref=volume.at[slab - 1, :, pl.ds(pl.multiple_of(strip * LANES, LANES), LANES)],
            dst_ref=vol.at[0, strip + 1, body, :],
            send_sem=front_sem.at[0, strip],
            recv_sem=front_sem.at[1, strip],
            device_id={"depth": lax.rem(me + 1, groups)},
            device_id_type=pl.DeviceIdType.MESH,
        )

    def back(strip):
        return pltpu.make_async_remote_copy(
            src_ref=volume.at[0, :, pl.ds(pl.multiple_of(strip * LANES, LANES), LANES)],
            dst_ref=vol.at[slab + 1, strip + 1, body, :],
            send_sem=back_sem.at[0, strip],
            recv_sem=back_sem.at[1, strip],
            device_id={"depth": lax.rem(me + groups - 1, groups)},
            device_id_type=pl.DeviceIdType.MESH,
        )

    def row_copy(src, dst, way, target):
        return pltpu.make_async_remote_copy(
            src_ref=src,
            dst_ref=dst,
            send_sem=row_sem.at[0, way],
            recv_sem=row_sem.at[1, way],
            device_id={"tile": target},
            device_id_type=pl.DeviceIdType.MESH,
        )

    def piece(strip, target, source, k):
        return pltpu.make_async_remote_copy(
            src_ref=sent.at[strip],
            dst_ref=got.at[source, :, :, pl.ds(pl.multiple_of(k * LANES, LANES), LANES)],
            send_sem=piece_send.at[strip],
            recv_sem=piece_recv.at[source, k],
            device_id={"depth": target},
            device_id_type=pl.DeviceIdType.MESH,
        )

    def own_copy(strip, k):
        return pltpu.make_async_copy(
            sent.at[strip], got.at[me, :, :, pl.ds(pl.multiple_of(k * LANES, LANES), LANES)], own_sem.at[k]
        )

    relays = own // 2 if groups == 4 else 0
    middle = jnp.logical_and(me > 0, me < groups - 1)

    def pass_in(strip, k):
        return pltpu.make_async_remote_copy(
            src_ref=sent.at[strip],
            dst_ref=passing.at[k],
            send_sem=piece_send.at[strip],
            recv_sem=pass_recv.at[k],
            device_id={"depth": lax.rem(me + 2, groups)},
            device_id_type=pl.DeviceIdType.MESH,
        )

    def pass_on(k):
        target = jnp.where(me == 0, 1, 2)
        source = 3 - target
        return pltpu.make_async_remote_copy(
            src_ref=passing.at[k],
            dst_ref=got.at[source, :, :, pl.ds(pl.multiple_of(k * LANES, LANES), LANES)],
            send_sem=pass_send.at[k],
            recv_sem=piece_recv.at[source, k],
            device_id={"depth": target},
            device_id_type=pl.DeviceIdType.MESH,
        )

    def strip_at(step, device):
        others = groups - 1
        away = step < own * others
        k = jnp.where(away, step // others, step - own * others)
        target = lax.rem(device + jnp.where(away, 1 + lax.rem(step, others), 0), groups)
        return target * own + k, target, k

    up, down = lax.rem(tile + tiles - 1, tiles), lax.rem(tile + 1, tiles)
    to_lower = row_copy(bottom_out, top_in, 0, down)
    to_upper = row_copy(top_out, bottom_in, 1, up)

    small = [
        pltpu.make_async_copy(src, dst, small_sem.at[i])
        for i, (src, dst) in enumerate(((entry_hbm, entry), (light_hbm, light), (transfer_hbm, transfer)))
    ]

    @pl.loop(0, strips)
    def _(strip):
        load(strip).start()

    for copy in small:
        copy.start()

    barrier = pltpu.get_barrier_semaphore()
    for hop in range(1, groups):
        pl.semaphore_signal(barrier, inc=1, device_id={"depth": lax.rem(me + hop, groups)},
                            device_id_type=pl.DeviceIdType.MESH)
    for target in (up, down):
        pl.semaphore_signal(barrier, inc=1, device_id={"tile": target}, device_id_type=pl.DeviceIdType.MESH)
    pl.semaphore_wait(barrier, groups + 1)

    @pl.loop(0, strips)
    def _(step):
        @pl.when(me < groups - 1)
        def _():
            front(strip_at(step, me + 1)[0]).start()

        @pl.when(me > 0)
        def _():
            back(strip_at(step, me - 1 + groups)[0]).start()

    zeros = jnp.zeros((rows, LANES), jnp.float32)

    @pl.when(me == 0)
    def _():
        @pl.loop(0, strips)
        def _(strip):
            vol[0, strip + 1, body, :] = zeros

    @pl.when(me == groups - 1)
    def _():
        @pl.loop(0, strips)
        def _(strip):
            vol[slab + 1, strip + 1, body, :] = zeros

    @pl.loop(0, slab)
    def _(layer):
        vol[layer + 1, 0, body, :] = zeros
        vol[layer + 1, strips + 1, body, :] = zeros

    @pl.loop(0, strips)
    def _(strip):
        load(strip).wait()
        for layer in range(slab):
            top_out[strip, pl.ds(layer, 1), :] = vol[layer + 1, strip + 1, pl.ds(PAD, 1), :]
            bottom_out[strip, pl.ds(layer, 1), :] = vol[layer + 1, strip + 1, pl.ds(PAD + rows - 1, 1), :]

    @pl.when(tile < tiles - 1)
    def _():
        to_lower.start()

    @pl.when(tile > 0)
    def _():
        to_upper.start()

    @pl.when(tile == 0)
    def _():
        top_in[...] = jnp.zeros_like(top_in)

    @pl.when(tile == tiles - 1)
    def _():
        bottom_in[...] = jnp.zeros_like(bottom_in)

    @pl.when(tile > 0)
    def _():
        to_lower.wait_recv()

    @pl.when(tile < tiles - 1)
    def _():
        to_upper.wait_recv()

    @pl.loop(0, strips)
    def _(strip):
        for layer in range(slab):
            vol[layer + 1, strip + 1, pl.ds(PAD - 1, 1), :] = top_in[strip, pl.ds(layer, 1), :]
            vol[layer + 1, strip + 1, pl.ds(PAD + rows, 1), :] = bottom_in[strip, pl.ds(layer, 1), :]

    for copy in small:
        copy.wait()

    shape = (BLOCK, LANES)
    light_sq = light[0] * light[0] + light[1] * light[1] + light[2] * light[2]
    light_scale = 0.35 * lax.rsqrt(jnp.full(shape, light_sq, jnp.float32))
    light_z, light_x, light_y = (light[i] * light_scale for i in range(3))
    halves = (0.5, 0.25, 0.5)
    tone = [[halves[j] * transfer[k, j] for j in range(3)] for k in range(3)]
    peak = 4.0 / depth_total
    thick = [-LOG2E * transfer[3, 0], -0.5 * LOG2E * transfer[3, 1], -LOG2E * transfer[3, 2] - math.log2(peak)]
    lane = lax.broadcasted_iota(jnp.int32, shape, 1)
    first, last = lane == 0, lane == LANES - 1

    @pl.loop(0, strips)
    def _(step):
        strip, target, k = strip_at(step, me)
        at = strip + 1

        @pl.when(me > 0)
        def _():
            front(strip).wait_recv()

        @pl.when(me < groups - 1)
        def _():
            back(strip).wait_recv()

        for low in range(0, rows, BLOCK):
            here = pl.ds(PAD + low, BLOCK)
            entered = entry[pl.ds(low, BLOCK), pl.ds(pl.multiple_of(strip * LANES, LANES), LANES)] - me * slab
            before, value = vol[0, at, here, :], vol[1, at, here, :]
            clear = jnp.ones(shape, jnp.float32)
            total = jnp.zeros(shape, jnp.float32)
            base = jnp.zeros(shape, jnp.float32)
            sums = [jnp.zeros(shape, jnp.float32)] * 3
            for layer in range(slab):
                after = vol[layer + 2, at, here, :]
                grad_z = after - before
                grad_x = vol[layer + 1, at, pl.ds(PAD + low + 1, BLOCK), :] - vol[
                    layer + 1, at, pl.ds(PAD + low - 1, BLOCK), :]
                right = jnp.where(first, vol[layer + 1, at + 1, here, :], value)
                left = jnp.where(last, vol[layer + 1, at - 1, here, :], value)
                grad_y = pltpu.roll(right, LANES - 1, 1) - pltpu.roll(left, 1, 1)
                square = (grad_z * grad_z + grad_x * grad_x) + (grad_y * grad_y + 4.0)
                inverse = lax.rsqrt(square)
                norm = square * inverse
                facing = jnp.abs(light_z * grad_z + light_x * grad_x + light_y * grad_y)
                half_shade = 0.15 + facing * inverse
                spread = 1.0 / peak + jnp.exp2(jnp.minimum(thick[0] * value + thick[1] * norm + thick[2], 126.0))
                guess = pl.reciprocal(spread, approx=True)
                opacity = guess * (2.0 - spread * guess)
                opacity = jnp.where(entered <= layer, opacity, 0.0)
                weight = clear * opacity
                clear = clear - weight
                total = total + weight
                lit = weight * half_shade
                base = base + lit
                for c in range(3):
                    sums[c] = sums[c] + lit * jnp.tanh(tone[c][0] * value + tone[c][1] * norm + tone[c][2])
                before, value = value, after
            for c in range(3):
                sent[strip, c, pl.ds(low, BLOCK), :] = base + sums[c]
            sent[strip, 3, pl.ds(low, BLOCK), :] = total

        relayed = jnp.logical_and(jnp.logical_and(middle, target == 3 - me), k < relays)

        @pl.when(jnp.logical_and(target != me, jnp.logical_not(relayed)))
        def _():
            piece(strip, target, me, k).start()

        if relays:
            @pl.when(relayed)
            def _():
                pass_in(strip, k).start()

            @pl.when(jnp.logical_and(jnp.logical_not(middle), jnp.logical_and(target == lax.rem(me + 1, groups), k >= own - relays)))
            def _():
                pass_in(strip, k - (own - relays)).wait_recv()
                pass_on(k - (own - relays)).start()

        @pl.when(target == me)
        def _():
            own_copy(strip, k).start()

    for k in range(own):
        own_copy(me * own + k, k).wait()
        for hop in range(1, groups):
            source = lax.rem(me + hop, groups)
            piece(source * own + k, source, source, k).wait_recv()

    @pl.loop(0, strips)
    def _(step):
        strip, target, k = strip_at(step, me)

        @pl.when(me < groups - 1)
        def _():
            front(strip).wait_send()

        @pl.when(me > 0)
        def _():
            back(strip).wait_send()

        @pl.when(target != me)
        def _():
            piece(strip, target, me, k).wait_send()

    if relays:
        @pl.when(jnp.logical_not(middle))
        def _():
            for k in range(relays):
                pass_on(k).wait_send()

    @pl.when(tile < tiles - 1)
    def _():
        to_lower.wait_send()

    @pl.when(tile > 0)
    def _():
        to_upper.wait_send()


def local(volume, entry_depth, light_dir, transfer):
    slab, rows, columns = volume.shape
    groups, tiles = lax.axis_size("depth"), lax.axis_size("tile")
    strips = columns // LANES
    own = strips // groups
    edge = pltpu.VMEM((strips, slab, LANES), jnp.float32)
    got = pl.pallas_call(
        functools.partial(kernel, groups, tiles, float(slab * groups)),
        out_shape=jax.ShapeDtypeStruct((groups, 4, rows, columns // groups), jnp.float32),
        in_specs=[pl.BlockSpec(memory_space=pl.ANY)] * 4,
        out_specs=pl.BlockSpec(memory_space=pl.ANY),
        scratch_shapes=[
            pltpu.VMEM((rows, columns), jnp.int32),
            pltpu.SMEM((3,), jnp.float32),
            pltpu.SMEM((4, 3), jnp.float32),
            pltpu.VMEM((slab + 2, strips + 2, rows + 2 * PAD, LANES), jnp.float32),
            edge,
            edge,
            edge,
            edge,
            pltpu.VMEM((strips, 4, rows, LANES), jnp.float32),
            pltpu.VMEM((max(own // 2, 1), 4, rows, LANES), jnp.float32),
            pltpu.SemaphoreType.DMA((3,)),
            pltpu.SemaphoreType.DMA((strips,)),
            pltpu.SemaphoreType.DMA((2, strips)),
            pltpu.SemaphoreType.DMA((2, strips)),
            pltpu.SemaphoreType.DMA((2, 2)),
            pltpu.SemaphoreType.DMA((strips,)),
            pltpu.SemaphoreType.DMA((groups, own)),
            pltpu.SemaphoreType.DMA((max(own // 2, 1),)),
            pltpu.SemaphoreType.DMA((max(own // 2, 1),)),
            pltpu.SemaphoreType.DMA((own,)),
        ],
        compiler_params=pltpu.CompilerParams(
            collective_id=0, has_side_effects=True, vmem_limit_bytes=60 * 1024 * 1024
        ),
        cost_estimate=pl.CostEstimate(
            flops=60 * slab * rows * columns, bytes_accessed=4 * slab * rows * columns, transcendentals=6 * slab * rows * columns
        ),
    )(volume, entry_depth, light_dir, transfer)
    frame, clear = got[0], 1.0 - got[0, 3]
    for source in range(1, groups):
        frame = frame + clear * got[source]
        clear = clear * (1.0 - got[source, 3])
    return frame


def solution(mesh):
    placed = (P("depth", "tile", None), P("tile", None), P(), P())
    return jax.shard_map(
        local, mesh=mesh, in_specs=placed, out_specs=P(None, "tile", "depth"), check_vma=False
    )
```

```python
import functools
import math

import jax
import jax.numpy as jnp
from jax import lax
from jax.experimental import pallas as pl
from jax.experimental.pallas import tpu as pltpu
from jax.sharding import PartitionSpec as P

LANES = 128
PAD = 8
BLOCK = 16
LOG2E = 1.4426950408889634


def kernel(groups, tiles, depth_total, volume, entry_hbm, light_hbm, transfer_hbm, out, entry, light, transfer, vol, top_out, bottom_out, top_in,
           bottom_in, sent, got, passing, detour, small_sem, load_sem, front_sem, back_sem, row_sem, piece_send, piece_recv, pass_send, pass_recv, hop_sem):
    slab, rows, columns = volume.shape
    strips = columns // LANES
    own = strips // groups
    me, tile = lax.axis_index("depth"), lax.axis_index("tile")
    body = pl.ds(PAD, rows)

    def load(strip):
        return pltpu.make_async_copy(
            volume.at[:, :, pl.ds(pl.multiple_of(strip * LANES, LANES), LANES)],
            vol.at[pl.ds(1, slab), strip + 1, body, :],
            load_sem.at[strip],
        )

    def front(strip):
        return pltpu.make_async_remote_copy(
            src_ref=volume.at[slab - 1, :, pl.ds(pl.multiple_of(strip * LANES, LANES), LANES)],
            dst_ref=vol.at[0, strip + 1, body, :],
            send_sem=front_sem.at[0, strip],
            recv_sem=front_sem.at[1, strip],
            device_id={"depth": lax.rem(me + 1, groups)},
            device_id_type=pl.DeviceIdType.MESH,
        )

    def back(strip):
        return pltpu.make_async_remote_copy(
            src_ref=volume.at[0, :, pl.ds(pl.multiple_of(strip * LANES, LANES), LANES)],
            dst_ref=vol.at[slab + 1, strip + 1, body, :],
            send_sem=back_sem.at[0, strip],
            recv_sem=back_sem.at[1, strip],
            device_id={"depth": lax.rem(me + groups - 1, groups)},
            device_id_type=pl.DeviceIdType.MESH,
        )

    def row_copy(src, dst, way, target):
        return pltpu.make_async_remote_copy(
            src_ref=src,
            dst_ref=dst,
            send_sem=row_sem.at[0, way],
            recv_sem=row_sem.at[1, way],
            device_id={"tile": target},
            device_id_type=pl.DeviceIdType.MESH,
        )

    def piece(strip, target, source, k):
        return pltpu.make_async_remote_copy(
            src_ref=sent.at[strip],
            dst_ref=got.at[source, k],
            send_sem=piece_send.at[strip],
            recv_sem=piece_recv.at[source, k],
            device_id={"depth": target},
            device_id_type=pl.DeviceIdType.MESH,
        )

    relays, detours = 0, strips // 2 if groups == 4 else 0
    middle = jnp.logical_and(me > 0, me < groups - 1)

    def pass_in(strip, k):
        return pltpu.make_async_remote_copy(
            src_ref=sent.at[strip],
            dst_ref=passing.at[k],
            send_sem=piece_send.at[strip],
            recv_sem=pass_recv.at[k],
            device_id={"depth": lax.rem(me + 2, groups)},
            device_id_type=pl.DeviceIdType.MESH,
        )

    def pass_on(k):
        target = jnp.where(me == 0, 1, 2)
        source = 3 - target
        return pltpu.make_async_remote_copy(
            src_ref=passing.at[k],
            dst_ref=got.at[source, k],
            send_sem=pass_send.at[k],
            recv_sem=piece_recv.at[source, k],
            device_id={"depth": target},
            device_id_type=pl.DeviceIdType.MESH,
        )

    across, mate = lax.rem(me + 2, groups), me + 1 - 2 * lax.rem(me, 2)
    outer = jnp.logical_not(middle)

    def detour_in(step):
        strip = strip_at(step, groups - 1 - me)[0]
        slot = step - (strips - detours)
        return pltpu.make_async_remote_copy(
            src_ref=volume.at[jnp.where(me == 1, slab - 1, 0), :, pl.ds(pl.multiple_of(strip * LANES, LANES), LANES)],
            dst_ref=detour.at[slot],
            send_sem=hop_sem.at[0, slot],
            recv_sem=hop_sem.at[1, slot],
            device_id={"depth": across},
            device_id_type=pl.DeviceIdType.MESH,
        )

    def detour_on(step, layer, sem):
        strip = strip_at(step, mate)[0]
        slot = step - (strips - detours)
        return pltpu.make_async_remote_copy(
            src_ref=detour.at[slot],
            dst_ref=vol.at[layer, strip + 1, body, :],
            send_sem=hop_sem.at[2, slot],
            recv_sem=sem.at[1, strip],
            device_id={"depth": mate},
            device_id_type=pl.DeviceIdType.MESH,
        )

    def halo_ways(step):
        ahead, behind = me < groups - 1, me > 0
        if not detours:
            return ahead, behind
        early = step < strips - detours
        return (
            jnp.logical_and(ahead, jnp.logical_or(early, me != 1)),
            jnp.logical_and(behind, jnp.logical_or(early, me != 2)),
        )

    def strip_at(step, device):
        others = groups - 1
        away = step < own * others
        k = jnp.where(away, step // others, step - own * others)
        target = lax.rem(device + jnp.where(away, 1 + lax.rem(step, others), 0), groups)
        return target * own + k, target, k

    up, down = lax.rem(tile + tiles - 1, tiles), lax.rem(tile + 1, tiles)
    to_lower = row_copy(bottom_out, top_in, 0, down)
    to_upper = row_copy(top_out, bottom_in, 1, up)

    small = [
        pltpu.make_async_copy(src, dst, small_sem.at[i])
        for i, (src, dst) in enumerate(((entry_hbm, entry), (light_hbm, light), (transfer_hbm, transfer)))
    ]

    @pl.loop(0, strips)
    def _(strip):
        load(strip).start()

    for copy in small:
        copy.start()

    barrier = pltpu.get_barrier_semaphore()
    for hop in range(1, groups):
        pl.semaphore_signal(barrier, inc=1, device_id={"depth": lax.rem(me + hop, groups)},
                            device_id_type=pl.DeviceIdType.MESH)
    for target in (up, down):
        pl.semaphore_signal(barrier, inc=1, device_id={"tile": target}, device_id_type=pl.DeviceIdType.MESH)
    pl.semaphore_wait(barrier, groups + 1)

    @pl.loop(0, strips)
    def _(step):
        ahead, behind = halo_ways(step)

        @pl.when(ahead)
        def _():
            front(strip_at(step, me + 1)[0]).start()

        @pl.when(behind)
        def _():
            back(strip_at(step, me - 1 + groups)[0]).start()

        if detours:
            @pl.when(jnp.logical_and(middle, step >= strips - detours))
            def _():
                detour_in(step).start()

    zeros = jnp.zeros((rows, LANES), jnp.float32)

    @pl.when(me == 0)
    def _():
        @pl.loop(0, strips)
        def _(strip):
            vol[0, strip + 1, body, :] = zeros

    @pl.when(me == groups - 1)
    def _():
        @pl.loop(0, strips)
        def _(strip):
            vol[slab + 1, strip + 1, body, :] = zeros

    @pl.loop(0, slab)
    def _(layer):
        vol[layer + 1, 0, body, :] = zeros
        vol[layer + 1, strips + 1, body, :] = zeros

    @pl.loop(0, strips)
    def _(strip):
        load(strip).wait()
        for layer in range(slab):
            top_out[strip, pl.ds(layer, 1), :] = vol[layer + 1, strip + 1, pl.ds(PAD, 1), :]
            bottom_out[strip, pl.ds(layer, 1), :] = vol[layer + 1, strip + 1, pl.ds(PAD + rows - 1, 1), :]

    @pl.when(tile < tiles - 1)
    def _():
        to_lower.start()

    @pl.when(tile > 0)
    def _():
        to_upper.start()

    @pl.when(tile == 0)
    def _():
        top_in[...] = jnp.zeros_like(top_in)

    @pl.when(tile == tiles - 1)
    def _():
        bottom_in[...] = jnp.zeros_like(bottom_in)

    @pl.when(tile > 0)
    def _():
        to_lower.wait_recv()

    @pl.when(tile < tiles - 1)
    def _():
        to_upper.wait_recv()

    @pl.loop(0, strips)
    def _(strip):
        for layer in range(slab):
            vol[layer + 1, strip + 1, pl.ds(PAD - 1, 1), :] = top_in[strip, pl.ds(layer, 1), :]
            vol[layer + 1, strip + 1, pl.ds(PAD + rows, 1), :] = bottom_in[strip, pl.ds(layer, 1), :]

    for copy in small:
        copy.wait()

    if detours:
        @pl.when(outer)
        def _():
            @pl.loop(strips - detours, strips)
            def _(step):
                detour_in(step).wait_recv()

                @pl.when(me == 0)
                def _():
                    detour_on(step, slab + 1, back_sem).start()

                @pl.when(me != 0)
                def _():
                    detour_on(step, 0, front_sem).start()

    shape = (BLOCK, LANES)
    light_sq = light[0] * light[0] + light[1] * light[1] + light[2] * light[2]
    light_scale = 0.35 * lax.rsqrt(jnp.full(shape, light_sq, jnp.float32))
    light_z, light_x, light_y = (light[i] * light_scale for i in range(3))
    halves = (0.5, 0.25, 0.5)
    tone = [[halves[j] * transfer[k, j] for j in range(3)] for k in range(3)]
    peak = 4.0 / depth_total
    thick = [-LOG2E * transfer[3, 0], -0.5 * LOG2E * transfer[3, 1], -LOG2E * transfer[3, 2] - math.log2(peak)]
    lane = lax.broadcasted_iota(jnp.int32, shape, 1)
    first, last = lane == 0, lane == LANES - 1

    @pl.loop(0, strips)
    def _(step):
        strip, target, k = strip_at(step, me)
        at = strip + 1

        @pl.when(me > 0)
        def _():
            front(strip).wait_recv()

        @pl.when(me < groups - 1)
        def _():
            back(strip).wait_recv()

        for low in range(0, rows, BLOCK):
            here = pl.ds(PAD + low, BLOCK)
            entered = entry[pl.ds(low, BLOCK), pl.ds(pl.multiple_of(strip * LANES, LANES), LANES)] - me * slab
            before, value = vol[0, at, here, :], vol[1, at, here, :]
            clear = jnp.ones(shape, jnp.float32)
            total = jnp.zeros(shape, jnp.float32)
            base = jnp.zeros(shape, jnp.float32)
            sums = [jnp.zeros(shape, jnp.float32)] * 3
            for layer in range(slab):
                after = vol[layer + 2, at, here, :]
                grad_z = after - before
                grad_x = vol[layer + 1, at, pl.ds(PAD + low + 1, BLOCK), :] - vol[
                    layer + 1, at, pl.ds(PAD + low - 1, BLOCK), :]
                right = jnp.where(first, vol[layer + 1, at + 1, here, :], value)
                left = jnp.where(last, vol[layer + 1, at - 1, here, :], value)
                grad_y = pltpu.roll(right, LANES - 1, 1) - pltpu.roll(left, 1, 1)
                square = (grad_z * grad_z + grad_x * grad_x) + (grad_y * grad_y + 4.0)
                inverse = lax.rsqrt(square)
                norm = square * inverse
                facing = jnp.abs(light_z * grad_z + light_x * grad_x + light_y * grad_y)
                half_shade = 0.15 + facing * inverse
                spread = 1.0 / peak + jnp.exp2(jnp.minimum(thick[0] * value + thick[1] * norm + thick[2], 126.0))
                guess = pl.reciprocal(spread, approx=True)
                opacity = guess * (2.0 - spread * guess)
                opacity = jnp.where(entered <= layer, opacity, 0.0)
                weight = clear * opacity
                clear = clear - weight
                total = total + weight
                lit = weight * half_shade
                base = base + lit
                for c in range(3):
                    sums[c] = sums[c] + lit * jnp.tanh(tone[c][0] * value + tone[c][1] * norm + tone[c][2])
                before, value = value, after
            for c in range(3):
                sent[strip, c, pl.ds(low, BLOCK), :] = base + sums[c]
            sent[strip, 3, pl.ds(low, BLOCK), :] = total

        relayed = jnp.logical_and(jnp.logical_and(middle, target == 3 - me), k < relays)

        @pl.when(jnp.logical_and(target != me, jnp.logical_not(relayed)))
        def _():
            piece(strip, target, me, k).start()

        if relays:
            @pl.when(relayed)
            def _():
                pass_in(strip, k).start()

            @pl.when(jnp.logical_and(jnp.logical_not(middle), jnp.logical_and(target == lax.rem(me + 1, groups), k >= own - relays)))
            def _():
                pass_in(strip, k - (own - relays)).wait_recv()
                pass_on(k - (own - relays)).start()

        @pl.when(target == me)
        def _():
            got[me, k] = sent[strip]

    for k in range(own):
        for hop in range(1, groups):
            source = lax.rem(me + hop, groups)
            piece(source * own + k, source, source, k).wait_recv()
        for low in range(0, rows, BLOCK):
            here = pl.ds(low, BLOCK)
            clear = jnp.ones(shape, jnp.float32)
            sums = [jnp.zeros(shape, jnp.float32)] * 4
            for source in range(groups):
                alpha = got[source, k, 3, here, :]
                for c in range(3):
                    sums[c] = sums[c] + clear * got[source, k, c, here, :]
                sums[3] = sums[3] + clear * alpha
                clear = clear - clear * alpha
            for c in range(4):
                out[c, here, pl.ds(k * LANES, LANES)] = sums[c]

    @pl.loop(0, strips)
    def _(step):
        strip, target, k = strip_at(step, me)

        ahead, behind = halo_ways(step)

        @pl.when(ahead)
        def _():
            front(strip_at(step, me + 1)[0]).wait_send()

        @pl.when(behind)
        def _():
            back(strip_at(step, me - 1 + groups)[0]).wait_send()

        if detours:
            @pl.when(jnp.logical_and(middle, step >= strips - detours))
            def _():
                detour_in(step).wait_send()

            @pl.when(jnp.logical_and(outer, step >= strips - detours))
            def _():
                detour_on(step, 0, front_sem).wait_send()

        @pl.when(target != me)
        def _():
            piece(strip, target, me, k).wait_send()

    if relays:
        @pl.when(jnp.logical_not(middle))
        def _():
            for k in range(relays):
                pass_on(k).wait_send()

    @pl.when(tile < tiles - 1)
    def _():
        to_lower.wait_send()

    @pl.when(tile > 0)
    def _():
        to_upper.wait_send()


def local(volume, entry_depth, light_dir, transfer):
    slab, rows, columns = volume.shape
    groups, tiles = lax.axis_size("depth"), lax.axis_size("tile")
    strips = columns // LANES
    own = strips // groups
    edge = pltpu.VMEM((strips, slab, LANES), jnp.float32)
    return pl.pallas_call(
        functools.partial(kernel, groups, tiles, float(slab * groups)),
        out_shape=jax.ShapeDtypeStruct((4, rows, columns // groups), jnp.float32),
        in_specs=[pl.BlockSpec(memory_space=pl.ANY)] * 4,
        out_specs=pl.BlockSpec(memory_space=pltpu.VMEM),
        scratch_shapes=[
            pltpu.VMEM((rows, columns), jnp.int32),
            pltpu.SMEM((3,), jnp.float32),
            pltpu.SMEM((4, 3), jnp.float32),
            pltpu.VMEM((slab + 2, strips + 2, rows + 2 * PAD, LANES), jnp.float32),
            edge,
            edge,
            edge,
            edge,
            pltpu.VMEM((strips, 4, rows, LANES), jnp.float32),
            pltpu.VMEM((groups, own, 4, rows, LANES), jnp.float32),
            pltpu.VMEM((max(own // 2, 1), 4, rows, LANES), jnp.float32),
            pltpu.VMEM((strips // 2, rows, LANES), jnp.float32),
            pltpu.SemaphoreType.DMA((3,)),
            pltpu.SemaphoreType.DMA((strips,)),
            pltpu.SemaphoreType.DMA((2, strips)),
            pltpu.SemaphoreType.DMA((2, strips)),
            pltpu.SemaphoreType.DMA((2, 2)),
            pltpu.SemaphoreType.DMA((strips,)),
            pltpu.SemaphoreType.DMA((groups, own)),
            pltpu.SemaphoreType.DMA((max(own // 2, 1),)),
            pltpu.SemaphoreType.DMA((max(own // 2, 1),)),
            pltpu.SemaphoreType.DMA((3, strips // 2)),
        ],
        compiler_params=pltpu.CompilerParams(
            collective_id=0, has_side_effects=True, vmem_limit_bytes=60 * 1024 * 1024
        ),
        cost_estimate=pl.CostEstimate(
            flops=60 * slab * rows * columns, bytes_accessed=4 * slab * rows * columns, transcendentals=6 * slab * rows * columns
        ),
    )(volume, entry_depth, light_dir, transfer)


def solution(mesh):
    placed = (P("depth", "tile", None), P("tile", None), P(), P())
    return jax.shard_map(
        local, mesh=mesh, in_specs=placed, out_specs=P(None, "tile", "depth"), check_vma=False
    )
```

```python
import functools
import math

import jax
import jax.numpy as jnp
from jax import lax
from jax.experimental import pallas as pl
from jax.experimental.pallas import tpu as pltpu
from jax.sharding import PartitionSpec as P

LANES = 128
PAD = 8
BLOCK = 16
LOG2E = 1.4426950408889634


def kernel(groups, tiles, depth_total, volume, entry_hbm, light_hbm, transfer_hbm, out, entry, light, transfer, vol, top_out, bottom_out, top_in,
           bottom_in, sent, got, passing, small_sem, load_sem, front_sem, back_sem, row_sem, piece_send, piece_recv, pass_send, pass_recv):
    slab, rows, columns = volume.shape
    strips = columns // LANES
    own = strips // groups
    me, tile = lax.axis_index("depth"), lax.axis_index("tile")
    body = pl.ds(PAD, rows)

    def load(strip):
        return pltpu.make_async_copy(
            volume.at[:, :, pl.ds(pl.multiple_of(strip * LANES, LANES), LANES)],
            vol.at[pl.ds(1, slab), strip + 1, body, :],
            load_sem.at[strip],
        )

    def front(strip):
        return pltpu.make_async_remote_copy(
            src_ref=volume.at[slab - 1, :, pl.ds(pl.multiple_of(strip * LANES, LANES), LANES)],
            dst_ref=vol.at[0, strip + 1, body, :],
            send_sem=front_sem.at[0, strip],
            recv_sem=front_sem.at[1, strip],
            device_id={"depth": lax.rem(me + 1, groups)},
            device_id_type=pl.DeviceIdType.MESH,
        )

    def back(strip):
        return pltpu.make_async_remote_copy(
            src_ref=volume.at[0, :, pl.ds(pl.multiple_of(strip * LANES, LANES), LANES)],
            dst_ref=vol.at[slab + 1, strip + 1, body, :],
            send_sem=back_sem.at[0, strip],
            recv_sem=back_sem.at[1, strip],
            device_id={"depth": lax.rem(me + groups - 1, groups)},
            device_id_type=pl.DeviceIdType.MESH,
        )

    def row_copy(src, dst, way, target):
        return pltpu.make_async_remote_copy(
            src_ref=src,
            dst_ref=dst,
            send_sem=row_sem.at[0, way],
            recv_sem=row_sem.at[1, way],
            device_id={"tile": target},
            device_id_type=pl.DeviceIdType.MESH,
        )

    def piece(strip, target, source, k):
        return pltpu.make_async_remote_copy(
            src_ref=sent.at[strip],
            dst_ref=got.at[source, k],
            send_sem=piece_send.at[strip],
            recv_sem=piece_recv.at[source, k],
            device_id={"depth": target},
            device_id_type=pl.DeviceIdType.MESH,
        )

    relays = own // 2 if groups == 4 else 0
    middle = jnp.logical_and(me > 0, me < groups - 1)

    def pass_in(strip, k):
        return pltpu.make_async_remote_copy(
            src_ref=sent.at[strip],
            dst_ref=passing.at[k],
            send_sem=piece_send.at[strip],
            recv_sem=pass_recv.at[k],
            device_id={"depth": lax.rem(me + 2, groups)},
            device_id_type=pl.DeviceIdType.MESH,
        )

    def pass_on(k):
        target = jnp.where(me == 0, 1, 2)
        source = 3 - target
        return pltpu.make_async_remote_copy(
            src_ref=passing.at[k],
            dst_ref=got.at[source, k],
            send_sem=pass_send.at[k],
            recv_sem=piece_recv.at[source, k],
            device_id={"depth": target},
            device_id_type=pl.DeviceIdType.MESH,
        )

    def strip_at(step, device):
        k = step // groups
        target = lax.rem(device + 1 + lax.rem(step, groups), groups)
        return target * own + k, target, k

    up, down = lax.rem(tile + tiles - 1, tiles), lax.rem(tile + 1, tiles)
    to_lower = row_copy(bottom_out, top_in, 0, down)
    to_upper = row_copy(top_out, bottom_in, 1, up)

    small = [
        pltpu.make_async_copy(src, dst, small_sem.at[i])
        for i, (src, dst) in enumerate(((entry_hbm, entry), (light_hbm, light), (transfer_hbm, transfer)))
    ]

    @pl.loop(0, strips)
    def _(strip):
        load(strip).start()

    for copy in small:
        copy.start()

    barrier = pltpu.get_barrier_semaphore()
    for hop in range(1, groups):
        pl.semaphore_signal(barrier, inc=1, device_id={"depth": lax.rem(me + hop, groups)},
                            device_id_type=pl.DeviceIdType.MESH)
    for target in (up, down):
        pl.semaphore_signal(barrier, inc=1, device_id={"tile": target}, device_id_type=pl.DeviceIdType.MESH)
    pl.semaphore_wait(barrier, groups + 1)

    @pl.loop(0, strips)
    def _(step):
        @pl.when(me < groups - 1)
        def _():
            front(strip_at(step, me + 1)[0]).start()

        @pl.when(me > 0)
        def _():
            back(strip_at(step, me - 1 + groups)[0]).start()

    zeros = jnp.zeros((rows, LANES), jnp.float32)

    @pl.when(me == 0)
    def _():
        @pl.loop(0, strips)
        def _(strip):
            vol[0, strip + 1, body, :] = zeros

    @pl.when(me == groups - 1)
    def _():
        @pl.loop(0, strips)
        def _(strip):
            vol[slab + 1, strip + 1, body, :] = zeros

    @pl.loop(0, slab)
    def _(layer):
        vol[layer + 1, 0, body, :] = zeros
        vol[layer + 1, strips + 1, body, :] = zeros

    @pl.loop(0, strips)
    def _(strip):
        load(strip).wait()
        for layer in range(slab):
            top_out[strip, pl.ds(layer, 1), :] = vol[layer + 1, strip + 1, pl.ds(PAD, 1), :]
            bottom_out[strip, pl.ds(layer, 1), :] = vol[layer + 1, strip + 1, pl.ds(PAD + rows - 1, 1), :]

    @pl.when(tile < tiles - 1)
    def _():
        to_lower.start()

    @pl.when(tile > 0)
    def _():
        to_upper.start()

    @pl.when(tile == 0)
    def _():
        top_in[...] = jnp.zeros_like(top_in)

    @pl.when(tile == tiles - 1)
    def _():
        bottom_in[...] = jnp.zeros_like(bottom_in)

    @pl.when(tile > 0)
    def _():
        to_lower.wait_recv()

    @pl.when(tile < tiles - 1)
    def _():
        to_upper.wait_recv()

    @pl.loop(0, strips)
    def _(strip):
        for layer in range(slab):
            vol[layer + 1, strip + 1, pl.ds(PAD - 1, 1), :] = top_in[strip, pl.ds(layer, 1), :]
            vol[layer + 1, strip + 1, pl.ds(PAD + rows, 1), :] = bottom_in[strip, pl.ds(layer, 1), :]

    for copy in small:
        copy.wait()

    shape = (BLOCK, LANES)
    light_sq = light[0] * light[0] + light[1] * light[1] + light[2] * light[2]
    light_scale = 0.35 * lax.rsqrt(jnp.full(shape, light_sq, jnp.float32))
    light_z, light_x, light_y = (light[i] * light_scale for i in range(3))
    halves = (0.5, 0.25, 0.5)
    tone = [[halves[j] * transfer[k, j] for j in range(3)] for k in range(3)]
    peak = 4.0 / depth_total
    thick = [-LOG2E * transfer[3, 0], -0.5 * LOG2E * transfer[3, 1], -LOG2E * transfer[3, 2] - math.log2(peak)]
    lane = lax.broadcasted_iota(jnp.int32, shape, 1)
    first, last = lane == 0, lane == LANES - 1

    @pl.loop(0, strips)
    def _(step):
        strip, target, k = strip_at(step, me)
        at = strip + 1

        @pl.when(me > 0)
        def _():
            front(strip).wait_recv()

        @pl.when(me < groups - 1)
        def _():
            back(strip).wait_recv()

        for low in range(0, rows, BLOCK):
            here = pl.ds(PAD + low, BLOCK)
            entered = entry[pl.ds(low, BLOCK), pl.ds(pl.multiple_of(strip * LANES, LANES), LANES)] - me * slab
            before, value = vol[0, at, here, :], vol[1, at, here, :]
            clear = jnp.ones(shape, jnp.float32)
            total = jnp.zeros(shape, jnp.float32)
            base = jnp.zeros(shape, jnp.float32)
            sums = [jnp.zeros(shape, jnp.float32)] * 3
            for layer in range(slab):
                after = vol[layer + 2, at, here, :]
                grad_z = after - before
                grad_x = vol[layer + 1, at, pl.ds(PAD + low + 1, BLOCK), :] - vol[
                    layer + 1, at, pl.ds(PAD + low - 1, BLOCK), :]
                right = jnp.where(first, vol[layer + 1, at + 1, here, :], value)
                left = jnp.where(last, vol[layer + 1, at - 1, here, :], value)
                grad_y = pltpu.roll(right, LANES - 1, 1) - pltpu.roll(left, 1, 1)
                square = (grad_z * grad_z + grad_x * grad_x) + (grad_y * grad_y + 4.0)
                inverse = lax.rsqrt(square)
                norm = square * inverse
                facing = jnp.abs(light_z * grad_z + light_x * grad_x + light_y * grad_y)
                half_shade = 0.15 + facing * inverse
                spread = 1.0 / peak + jnp.exp2(jnp.minimum(thick[0] * value + thick[1] * norm + thick[2], 126.0))
                guess = pl.reciprocal(spread, approx=True)
                opacity = guess * (2.0 - spread * guess)
                opacity = jnp.where(entered <= layer, opacity, 0.0)
                weight = clear * opacity
                clear = clear - weight
                total = total + weight
                lit = weight * half_shade
                base = base + lit
                for c in range(3):
                    sums[c] = sums[c] + lit * jnp.tanh(tone[c][0] * value + tone[c][1] * norm + tone[c][2])
                before, value = value, after
            for c in range(3):
                sent[strip, c, pl.ds(low, BLOCK), :] = base + sums[c]
            sent[strip, 3, pl.ds(low, BLOCK), :] = total

        relayed = jnp.logical_and(jnp.logical_and(middle, target == 3 - me), k < relays)

        @pl.when(jnp.logical_and(target != me, jnp.logical_not(relayed)))
        def _():
            piece(strip, target, me, k).start()

        if relays:
            @pl.when(relayed)
            def _():
                pass_in(strip, k).start()

            @pl.when(jnp.logical_and(jnp.logical_not(middle), jnp.logical_and(lax.rem(step, groups) == 0, k >= own - relays)))
            def _():
                pass_in(strip, k - (own - relays)).wait_recv()
                pass_on(k - (own - relays)).start()

        @pl.when(target == me)
        def _():
            got[me, k] = sent[strip]

    for k in range(own):
        for hop in range(1, groups):
            source = lax.rem(me + hop, groups)
            piece(source * own + k, source, source, k).wait_recv()
        for low in range(0, rows, BLOCK):
            here = pl.ds(low, BLOCK)
            clear = jnp.ones(shape, jnp.float32)
            sums = [jnp.zeros(shape, jnp.float32)] * 4
            for source in range(groups):
                alpha = got[source, k, 3, here, :]
                for c in range(3):
                    sums[c] = sums[c] + clear * got[source, k, c, here, :]
                sums[3] = sums[3] + clear * alpha
                clear = clear - clear * alpha
            for c in range(4):
                out[c, here, pl.ds(k * LANES, LANES)] = sums[c]

    @pl.loop(0, strips)
    def _(step):
        strip, target, k = strip_at(step, me)

        @pl.when(me < groups - 1)
        def _():
            front(strip).wait_send()

        @pl.when(me > 0)
        def _():
            back(strip).wait_send()

        @pl.when(target != me)
        def _():
            piece(strip, target, me, k).wait_send()

    if relays:
        @pl.when(jnp.logical_not(middle))
        def _():
            for k in range(relays):
                pass_on(k).wait_send()

    @pl.when(tile < tiles - 1)
    def _():
        to_lower.wait_send()

    @pl.when(tile > 0)
    def _():
        to_upper.wait_send()


def local(volume, entry_depth, light_dir, transfer):
    slab, rows, columns = volume.shape
    groups, tiles = lax.axis_size("depth"), lax.axis_size("tile")
    strips = columns // LANES
    own = strips // groups
    edge = pltpu.VMEM((strips, slab, LANES), jnp.float32)
    return pl.pallas_call(
        functools.partial(kernel, groups, tiles, float(slab * groups)),
        out_shape=jax.ShapeDtypeStruct((4, rows, columns // groups), jnp.float32),
        in_specs=[pl.BlockSpec(memory_space=pl.ANY)] * 4,
        out_specs=pl.BlockSpec(memory_space=pltpu.VMEM),
        scratch_shapes=[
            pltpu.VMEM((rows, columns), jnp.int32),
            pltpu.SMEM((3,), jnp.float32),
            pltpu.SMEM((4, 3), jnp.float32),
            pltpu.VMEM((slab + 2, strips + 2, rows + 2 * PAD, LANES), jnp.float32),
            edge,
            edge,
            edge,
            edge,
            pltpu.VMEM((strips, 4, rows, LANES), jnp.float32),
            pltpu.VMEM((groups, own, 4, rows, LANES), jnp.float32),
            pltpu.VMEM((max(own // 2, 1), 4, rows, LANES), jnp.float32),
            pltpu.SemaphoreType.DMA((3,)),
            pltpu.SemaphoreType.DMA((strips,)),
            pltpu.SemaphoreType.DMA((2, strips)),
            pltpu.SemaphoreType.DMA((2, strips)),
            pltpu.SemaphoreType.DMA((2, 2)),
            pltpu.SemaphoreType.DMA((strips,)),
            pltpu.SemaphoreType.DMA((groups, own)),
            pltpu.SemaphoreType.DMA((max(own // 2, 1),)),
            pltpu.SemaphoreType.DMA((max(own // 2, 1),)),
        ],
        compiler_params=pltpu.CompilerParams(
            collective_id=0, has_side_effects=True, vmem_limit_bytes=60 * 1024 * 1024
        ),
        cost_estimate=pl.CostEstimate(
            flops=60 * slab * rows * columns, bytes_accessed=4 * slab * rows * columns, transcendentals=6 * slab * rows * columns
        ),
    )(volume, entry_depth, light_dir, transfer)


def solution(mesh):
    placed = (P("depth", "tile", None), P("tile", None), P(), P())
    return jax.shard_map(
        local, mesh=mesh, in_specs=placed, out_specs=P(None, "tile", "depth"), check_vma=False
    )
```
